128 devices in a mesh: ta: 16 (over z, x_hi, core), ha: 2 (over x_lo), wa: 4 (over y).
Axes of the slice: x: 4 (x_hi: 2, x_lo: 2; x = x_hi * 2 + x_lo), y: 4, z: 4, core: 2. Of those that a mesh axis runs over, the one named last changes fastest.
Arguments:
- video_in: float32 [64, 16, 64, 128], P('ta', 'ha', 'wa'), may hold values from -6 to 6
- first_filter: float32 [27, 128, 128], replicated, may hold values from -0.109375 to 0.109375
- first_bias: float32 [128], replicated, may hold values from -3 to 3
- second_filter: float32 [27, 128, 128], replicated, may hold values from -0.109375 to 0.109375
- grad_output: float32 [64, 16, 64, 128], P('ta', 'ha', 'wa'), may hold values from -8 to 8
Outputs:
- grad_input: float32 [64, 16, 64, 128], P('ta', 'ha', 'wa')
- grad_first: float32 [3456, 128], P('ta')
- grad_second: float32 [3456, 128], P('ta')
- grad_bias: float32 [128], replicated
The draws below stay inside these ranges and needn't reach their ends.
All inputs are finite; a program needn't handle non-finite values.
Results may differ from the reference program's by a relative error of at most 0.00018.
Values sent between devices are 32-bit elements; how exact they have to be, the bound alone decides.
A program may use at most 128 MiB of HBM per device.

```python
import jax
import jax.numpy as jnp
from jax import lax

C = 128
NT = 64
NH = 16
NW = 64


def draw_grad_output(key, part):
    key = jax.random.fold_in(key, 11)
    noise_key, offset_key = jax.random.split(key, 2)
    noise = jax.random.normal(noise_key, (NT, NH, NW, C), jnp.float32)
    offset = 0.1 * jax.random.normal(offset_key, (C,), jnp.float32)
    return jnp.clip(noise + offset, -6.0, 6.0)


def block_scale(rng, shape, cuts, low, top_value):
    gain, own = 1.0, jax.random.fold_in(rng, 6)
    for position, shards_of in cuts:
        heights = jnp.exp(jax.random.uniform(jax.random.fold_in(own, position), (shards_of,), jnp.float32, low / len(cuts), top_value / len(cuts)))
        gain = gain * jnp.repeat(heights, shape[position] // shards_of).reshape([-1 if axis == position else 1 for axis in range(len(shape))])
    return gain


def gaussian(stream_key, shape, deviation, most, cuts=(), dtype=jnp.bfloat16):
    drawn = deviation * jax.random.normal(stream_key, shape, jnp.float32)
    if cuts:
        drawn = drawn * block_scale(stream_key, shape, cuts, -0.22, 0.18)
    return jnp.clip(drawn, -most, most).astype(dtype)


def setup_inputs(seed: int = 0) -> dict:
    seeds = jax.random.split(jax.random.key(seed), 6)
    return {
        "video_in": gaussian(seeds[0], (NT, NH, NW, C), 1.0, 6.0, ((0, 16), (1, 2), (2, 4)), jnp.float32),
        "first_filter": gaussian(seeds[1], (27, C, C), (27 * C) ** -0.5, 0.109375, (), jnp.float32),
        "first_bias": gaussian(seeds[2], (C,), 0.5, 3.0, (), jnp.float32),
        "second_filter": gaussian(seeds[3], (27, C, C), (27 * C) ** -0.5, 0.109375, (), jnp.float32),
        "grad_output": draw_grad_output(jax.random.fold_in(seeds[5], 71), 0),
    }


def causal_conv(volume, filters):
    channels = filters.shape[-1]
    kernel = filters.reshape(3, 3, 3, channels, channels)
    result = lax.conv_general_dilated(volume[None], kernel, (1, 1, 1), [(2, 0), (1, 1), (1, 1)], dimension_numbers=('NDHWC', 'DHWIO', 'NDHWC'), precision=lax.Precision.HIGHEST)
    return result[0]

def forward(video_in, first_filter, first_bias, second_filter):
    pre = causal_conv(video_in, first_filter) + first_bias
    return causal_conv(jax.nn.silu(pre), second_filter)

def reference(video_in, first_filter, first_bias, second_filter, grad_output):
    outputs, pullback = jax.vjp(forward, video_in, first_filter, first_bias, second_filter)
    grad_input, raw_first, raw_bias, raw_second = pullback(grad_output)
    squares = jnp.sum(raw_first * raw_first) + jnp.sum(raw_second * raw_second) + jnp.sum(raw_bias * raw_bias)
    channels = first_filter.shape[-1]
    limit = jnp.sqrt(jnp.float32(54 * channels * channels + channels))
    factor = jnp.minimum(jnp.float32(1.0), limit / jnp.sqrt(squares))
    grad_first = (factor * raw_first).reshape(27 * channels, channels)
    grad_second = (factor * raw_second).reshape(27 * channels, channels)
    return (grad_input, grad_first, grad_second, factor * raw_bias)
```

```python
import jax
import jax.numpy as jnp
from jax import lax
from jax.experimental import pallas as pl
from jax.experimental.pallas import tpu as pltpu
from jax.sharding import PartitionSpec as P

f32, bf16 = jnp.float32, jnp.bfloat16
MESH = pl.DeviceIdType.MESH
C = 128
T, H, W = 4, 8, 16
V = T * H * W
ROWS = 27 * C
OWN = ROWS // 16
PAD = OWN + 8
HALF = PAD // 2
QUART = HALF // 2
LEFT = 8
LIMIT = float(54 * C * C + C)


def split(value):
    high = value.astype(bf16)
    low = (value - high.astype(f32)).astype(bf16)
    return high, low


def mod(value, count):
    return lax.rem(value + 2 * count, count)


def rows8(start, size):
    return pl.ds(pl.multiple_of(start, 8), size)


def remote(src, dst, send, recv, device):
    return pltpu.make_async_remote_copy(
        src_ref=src, dst_ref=dst, send_sem=send, recv_sem=recv, device_id=device,
        device_id_type=MESH,
    )


def kernel(
    video, first, bias, second, cot,
    grad_input, grad_first, grad_second, grad_bias,
    w_f32, w_split, ext, cols, cols_ext, shifted, acc, pre_ref, act_t, vid_t,
    raw, bias8, pack, core0, core1, rs1_0, rs1_1, rs2_0, rs2_1,
    tot, x_recv, tot2, tot3, full, note, notes,
    local_sem, halo_send, halo_recv, core_send, core_recv, rs_send, rs_recv,
    x_send, x_rcv, ag_send, ag_recv, n_send, n_recv,
):
    ta, ha, wa = lax.axis_index("ta"), lax.axis_index("ha"), lax.axis_index("wa")
    core = lax.rem(ta, 2)
    x_hi = lax.rem(ta // 2, 2)
    z = ta // 4
    y = wa
    other = 1 - ha

    own_at = (2, 0, 0)
    blocks = [
        pltpu.make_async_copy(
            src, ext.at[n, pl.ds(own_at[n], T), pl.ds(1, H), pl.ds(LEFT, W)], local_sem.at[n]
        )
        for n, src in enumerate((video, cot))
    ]
    loads = [
        pltpu.make_async_copy(src, w_f32.at[n], local_sem.at[2 + n])
        for n, src in enumerate((first, second))
    ]
    for copy in blocks + loads:
        copy.start()

    gap = 9 * ha
    for n in range(3):
        ext[n, :, pl.ds(gap, 1)] = jnp.zeros((T + 2, 1, 32, C), f32)
        cols_ext[n, :, :, pl.ds(gap, 1)] = jnp.zeros((2, T + 2, 1, 1, C), f32)

    barrier = pltpu.get_barrier_semaphore()
    greeted = []
    for dt in (-1, 0, 1):
        for row in (ha, other):
            for dw in (-1, 0, 1):
                if not (dt == 0 and row is ha and dw == 0):
                    greeted.append((mod(ta + dt, 16), row, mod(wa + dw, 4)))
    for step in range(2, 15):
        greeted.append((mod(ta + step, 16), ha, wa))
    greeted.append((ta, ha, mod(wa + 2, 4)))
    flip2 = ta + 2 - 4 * x_hi
    greeted.append((flip2, other, wa))
    for device in greeted:
        pl.semaphore_signal(barrier, inc=1, device_id=device, device_id_type=MESH)
    pl.semaphore_wait(barrier, len(greeted))

    halo_at = (0, 4, 4)
    edge_at = (2, 0, 0)
    along = (1, -1, -1)
    edge_row = 7 * other

    def halo_plain(n, src):
        copies = []
        for slot, (dt, dh) in enumerate(((0, 1), (1, 0), (1, 1))):
            frames = pl.ds(edge_at[n], 2) if dt else pl.ds(0, T)
            to = pl.ds(halo_at[n], 2) if dt else pl.ds(own_at[n], T)
            rows = pl.ds(edge_row, 1) if dh else pl.ds(0, H)
            to_rows = pl.ds(gap, 1) if dh else pl.ds(1, H)
            copies.append(
                remote(
                    src(frames, rows),
                    ext.at[n, to, to_rows, pl.ds(LEFT, W)],
                    halo_send.at[n, slot], halo_recv.at[n, slot],
                    (mod(ta + along[n] * dt, 16), other if dh else ha, wa),
                )
            )
        return copies

    def halo_columns(n):
        copies = []
        slot = 3
        for dt in (0, 1):
            for dh in (0, 1):
                for side, dw in ((0, -1), (1, 1)):
                    if dt + dh + abs(dw) == 0:
                        continue
                    frames = pl.ds(edge_at[n], 2) if dt else pl.ds(0, T)
                    to = pl.ds(halo_at[n], 2) if dt else pl.ds(own_at[n], T)
                    rows = pl.ds(edge_row, 1) if dh else pl.ds(0, H)
                    to_rows = pl.ds(gap, 1) if dh else pl.ds(1, H)
                    copies.append(
                        remote(
                            cols.at[n, side, frames, rows],
                            cols_ext.at[n, 1 - side, to, to_rows],
                            halo_send.at[n, slot], halo_recv.at[n, slot],
                            (mod(ta + along[n] * dt, 16), other if dh else ha, mod(wa + dw, 4)),
                        )
                    )
                    slot += 1
        return copies

    def pack_columns(n):
        own = ext[n, pl.ds(own_at[n], T), pl.ds(1, H), pl.ds(LEFT, W)]
        cols[n, 0] = own[:, :, 0:1]
        cols[n, 1] = own[:, :, W - 1 : W]

    plain = [halo_plain(0, lambda t, h: video.at[t, h]), halo_plain(1, lambda t, h: cot.at[t, h])]
    for copies in plain:
        for copy in copies:
            copy.start()
    strips = [halo_columns(0), halo_columns(1)]
    for n in (0, 1):
        blocks[n].wait()
        pack_columns(n)
        for copy in strips[n]:
            copy.start()

    for copy in loads:
        copy.wait()

    def split_filters(tap, _):
        for n in range(2):
            high, low = split(w_f32[n, tap])
            w_split[n, tap, :, :C] = high
            w_split[n, tap, :, C:] = low
        return 0

    lax.fori_loop(0, 27, split_filters, 0)

    def transposed(value, ref):
        high, low = split(value.T)
        ref[:C] = high
        ref[C:] = low

    transposed(ext[0, pl.ds(2, T), pl.ds(1, H), pl.ds(LEFT, W)].reshape(V, C), vid_t)

    left_in = (wa > 0).astype(f32)
    right_in = (wa < 3).astype(f32)
    frame_in = ((ta > 0).astype(f32), (ta < 15).astype(f32), (ta < 15).astype(f32))

    def shift_columns(n):
        def frame(t, _):
            ext[n, t, :, LEFT - 1 : LEFT] = cols_ext[n, 0, t] * left_in
            ext[n, t, :, LEFT + W : LEFT + W + 1] = cols_ext[n, 1, t] * right_in
            is_halo = jnp.logical_and(t >= halo_at[n], t < halo_at[n] + 2)
            keep = jnp.where(is_halo, frame_in[n], 1.0)
            for c in range(3):
                high, low = split(ext[n, t, :, LEFT - 1 + c : LEFT - 1 + c + W] * keep)
                shifted[n, c, t, :, :, :C] = high
                shifted[n, c, t, :, :, C:] = low
            return 0

        lax.fori_loop(0, T + 2, frame, 0)

    def conv(n, filters, back):
        for a in range(3):
            pieces, blocks_w = [], []
            for b in range(3):
                for c in range(3):
                    at = (2 - a, 2 - b, 2 - c) if back else (a, b, c)
                    window = shifted[n, at[2], pl.ds(at[0], T), pl.ds(at[1], H)]
                    pieces.append(window.reshape(V, 2 * C))
                    w = w_split[filters, 9 * a + 3 * b + c]
                    if back:
                        high, low = w[:, :C], w[:, C:]
                        blocks_w.append(
                            jnp.concatenate(
                                [
                                    jnp.concatenate([high, high], axis=1),
                                    jnp.concatenate([low, low], axis=1),
                                ],
                                axis=0,
                            )
                        )
                    else:
                        blocks_w += [w, w]
            columns = jnp.concatenate(pieces, axis=1)
            if back:
                product = lax.dot_general(
                    columns, jnp.concatenate(blocks_w, axis=1), (((1,), (1,)), ((), ())),
                    preferred_element_type=f32,
                )
            else:
                product = jnp.dot(
                    columns, jnp.concatenate(blocks_w, axis=0), preferred_element_type=f32
                )
            if a == 0:
                acc[...] = product
            else:
                acc[...] += product
        return acc[:, :C] + acc[:, C:]

    def weight_grad(fixed, n, f):
        def taps(step, _):
            a, b = step // 3, lax.rem(step, 3)
            for c in range(3):
                window = shifted[n, 2 - c, pl.ds(2 - a, T), pl.ds(2 - b, H)].reshape(V, 2 * C)
                o = jnp.dot(fixed[...], window, preferred_element_type=f32)
                raw[f, rows8((3 * step + c) * C, C)] = (o[:C, :C] + o[C:, :C]) + (
                    o[:C, C:] + o[C:, C:]
                )
            return 0

        lax.fori_loop(0, 9, taps, 0)

    for copy in plain[0] + strips[0]:
        copy.wait_recv()
    shift_columns(0)
    pre = conv(0, 0, False) + bias[...]
    pre_ref[...] = pre
    sig = 1.0 / (1.0 + jnp.exp(-pre))
    transposed(pre * sig, act_t)

    for copy in plain[1] + strips[1]:
        copy.wait_recv()
    shift_columns(1)
    grad_act = conv(1, 1, True)
    pre = pre_ref[...]
    sig = 1.0 / (1.0 + jnp.exp(-pre))
    grad_pre = grad_act * sig * (1.0 + pre * (1.0 - sig))
    bias8[...] = jnp.sum(grad_pre.reshape(V // 8, 8, C), axis=0)
    ext[2, pl.ds(0, T), pl.ds(1, H), pl.ds(LEFT, W)] = grad_pre.reshape(T, H, W, C)
    plain.append(
        halo_plain(2, lambda t, h: ext.at[2, t, pl.ds(h.start + 1, h.size), pl.ds(LEFT, W)])
    )
    for copy in plain[2]:
        copy.start()
    pack_columns(2)
    strips.append(halo_columns(2))
    for copy in strips[2]:
        copy.start()

    core_buf = (core0, core1)

    def owner(f, i, j):
        kz, kx = (i, j) if f == 0 else (j, i)
        return 4 * kz + 2 * kx

    def core_swap(f):
        outer, inner = (4, 2) if f == 0 else (2, 4)
        for i in range(outer):
            for j in range(inner):
                k = owner(f, i, j) + 1 - core
                pack[f, i * inner + j, :OWN] = raw[f, rows8(OWN * k, OWN)]
                pack[f, i * inner + j, OWN:] = bias8[...] if f else jnp.zeros((8, C), f32)
        copy = remote(
            pack.at[f], core_buf[f], core_send.at[f], core_recv.at[f],
            (ta + 1 - 2 * core, ha, wa),
        )
        copy.start()
        return copy

    def core_add(f):
        outer, inner = (4, 2) if f == 0 else (2, 4)
        for i in range(outer):
            for j in range(inner):
                k = owner(f, i, j) + core
                q = i * inner + j
                core_buf[f][q, :OWN] += raw[f, rows8(OWN * k, OWN)]
                if f:
                    core_buf[f][q, OWN:] += bias8[...]

    weight_grad(act_t, 1, 0)
    swap0 = core_swap(0)
    for copy in plain[2] + strips[2]:
        copy.wait_recv()
    shift_columns(2)
    weight_grad(vid_t, 2, 1)
    swap1 = core_swap(1)

    z_next, z_prev = (mod(ta + 4, 16), ha, wa), (mod(ta - 4, 16), ha, wa)
    y_next, y_prev = (ta, ha, mod(wa + 1, 4)), (ta, ha, mod(wa - 1, 4))

    def ring_start(s, i, nxt, prv, part, recv):
        copies = []
        for slot, (shard, half, device) in enumerate(
            ((2, 0, nxt), (1, 1, nxt), (2, 1, prv), (-1, 0, prv))
        ):
            copies.append(
                remote(
                    part(mod(i + shard, 4), half), recv.at[slot],
                    rs_send.at[s, slot], rs_recv.at[s, slot], device,
                )
            )
        for copy in copies:
            copy.start()
        return copies

    def ring_middle(s, i, nxt, prv, part, recv, copies):
        for slot, shard, half, device in ((0, 1, 0, nxt), (2, -1, 1, prv)):
            copies[slot].wait_recv()
            mine = part(mod(i + shard, 4), half)
            mine[...] += recv[slot]
            copy = remote(
                mine, recv.at[4 + slot // 2],
                rs_send.at[s, 4 + slot // 2], rs_recv.at[s, 4 + slot // 2], device,
            )
            copy.start()
            copies.append(copy)

    def ring_end(i, part, recv, copies, stores):
        for half, one, two in ((0, 3, 4), (1, 1, 5)):
            copies[one].wait_recv()
            copies[two].wait_recv()
            stores[half][...] = part(i, half)[...] + (recv[one] + recv[two])
        for copy in copies:
            copy.wait_send()

    def part1_0(shard, half):
        return core0.at[2 * shard + half]

    def part1_1(shard, half):
        return core1.at[
            pl.ds(4 * (shard // 2) + 2 * half, 2), rows8(lax.rem(shard, 2) * HALF, HALF)
        ]

    def part2_0(shard, half):
        return core0.at[
            2 * z + shard // 2, rows8(lax.rem(shard, 2) * HALF + half * QUART, QUART)
        ]

    def part2_1(shard, half):
        return core1.at[4 * (y // 2) + shard, rows8(lax.rem(y, 2) * HALF + half * QUART, QUART)]

    swap0.wait_recv()
    core_add(0)
    ring0 = ring_start(0, z, z_next, z_prev, part1_0, rs1_0)
    swap1.wait_recv()
    core_add(1)
    ring1 = ring_start(1, y, y_next, y_prev, part1_1, rs1_1)

    grad_input[...] = conv(2, 0, True).reshape(T, H, W, C)

    ring_middle(0, z, z_next, z_prev, part1_0, rs1_0, ring0)
    ring_middle(1, y, y_next, y_prev, part1_1, rs1_1, ring1)
    ring_end(z, part1_0, rs1_0, ring0, [part1_0(z, 0), part1_0(z, 1)])
    ring2 = ring_start(2, y, y_next, y_prev, part2_0, rs2_0)
    ring_end(y, part1_1, rs1_1, ring1, [part1_1(y, 0), part1_1(y, 1)])
    ring3 = ring_start(3, z, z_next, z_prev, part2_1, rs2_1)
    ring_middle(2, y, y_next, y_prev, part2_0, rs2_0, ring2)
    ring_middle(3, z, z_next, z_prev, part2_1, rs2_1, ring3)

    def tot_halves(f):
        return [tot.at[f, pl.ds(0, QUART)], tot.at[f, pl.ds(QUART, QUART)]]

    across = ((flip2, other, wa), (ta, other, wa))
    x_copies = []

    def x_start(step, f, src):
        copy = remote(
            src.at[f], x_recv.at[step, f], x_send.at[step, f], x_rcv.at[step, f], across[step]
        )
        copy.start()
        x_copies.append(copy)
        return copy

    ring_end(y, part2_0, rs2_0, ring2, tot_halves(0))
    first_x = [x_start(0, 0, tot)]
    ring_end(z, part2_1, rs2_1, ring3, tot_halves(1))
    first_x.append(x_start(0, 1, tot))
    second_x = []
    for f in range(2):
        first_x[f].wait_recv()
        tot2[f] = tot[f] + x_recv[0, f]
        second_x.append(x_start(1, f, tot2))
    for f in range(2):
        second_x[f].wait_recv()
        tot3[f] = tot2[f] + x_recv[1, f]

    holder = y // 2 == x_hi
    mine = lax.rem(y, 2)

    def shares():
        return [
            remote(
                tot3, full.at[mine], ag_send.at[step - 1], ag_recv.at[mine],
                (ta, ha, mod(wa + step, 4)),
            )
            for step in (1, 2, 3)
        ]

    @pl.when(holder)
    def _():
        for copy in shares():
            copy.start()
        full[mine] = tot3[...]

    for part in range(2):

        @pl.when(y != 2 * x_hi + part)
        def _(part=part):
            remote(
                tot3, full.at[part], ag_send.at[0], ag_recv.at[part], (ta, ha, mod(wa + 1, 4))
            ).wait_recv()

    squares = jnp.zeros((8, C), f32)
    for f in range(2):
        low, high = full[0, f], full[1, f, : OWN - HALF]
        squares += jnp.sum((low * low).reshape(-1, 8, C), axis=0)
        squares += jnp.sum((high * high).reshape(-1, 8, C), axis=0)
    note[:8] = squares
    note[8:] = full[1, 1, OWN - HALF :]
    notes[ta] = note[...]

    def tell(step):
        return remote(
            note, notes.at[ta], n_send.at[step], n_recv.at[ta], (mod(ta + step, 16), ha, wa)
        )

    def heard(step):
        source = mod(ta - step, 16)
        return remote(
            note, notes.at[source], n_send.at[step], n_recv.at[source], (source, ha, wa)
        )

    for step in range(1, 16):
        tell(step).start()
    for step in range(1, 16):
        heard(step).wait_recv()
    everything = jnp.sum(notes[:, :8], axis=0)
    raw_bias = jnp.sum(notes[0, 8:], axis=0, keepdims=True)
    norm2 = jnp.sum(everything, axis=(0, 1), keepdims=True) + jnp.sum(
        raw_bias * raw_bias, axis=(0, 1), keepdims=True
    )
    factor = jnp.minimum(1.0, jnp.sqrt(jnp.full((1, 1), LIMIT, f32)) / jnp.sqrt(norm2))
    for f, out in ((0, grad_second), (1, grad_first)):
        out[:HALF] = full[0, f] * factor
        out[HALF:] = full[1, f, : OWN - HALF] * factor
    grad_bias[...] = raw_bias * factor

    for copies in plain + strips:
        for copy in copies:
            copy.wait_send()
    swap0.wait_send()
    swap1.wait_send()
    for copy in x_copies:
        copy.wait_send()

    @pl.when(holder)
    def _():
        for copy in shares():
            copy.wait_send()

    for step in range(1, 16):
        tell(step).wait_send()


def per_device(video_in, first_filter, first_bias, second_filter, grad_output):
    vmem = pltpu.VMEM
    dma = pltpu.SemaphoreType.DMA
    any_spec = pl.BlockSpec(memory_space=pl.ANY)
    vmem_spec = pl.BlockSpec(memory_space=pltpu.VMEM)
    outs = pl.pallas_call(
        kernel,
        out_shape=(
            jax.ShapeDtypeStruct((T, H, W, C), f32),
            jax.ShapeDtypeStruct((OWN, C), f32),
            jax.ShapeDtypeStruct((OWN, C), f32),
            jax.ShapeDtypeStruct((1, C), f32),
        ),
        in_specs=[any_spec, any_spec, vmem_spec, any_spec, any_spec],
        out_specs=[vmem_spec] * 4,
        scratch_shapes=[
            vmem((2, 27, C, C), f32),
            vmem((2, 27, C, 2 * C), bf16),
            vmem((3, T + 2, H + 2, 32, C), f32),
            vmem((3, 2, T, H, 1, C), f32),
            vmem((3, 2, T + 2, H + 2, 1, C), f32),
            vmem((3, 3, T + 2, H + 2, W, 2 * C), bf16),
            vmem((V, 2 * C), f32),
            vmem((V, C), f32),
            vmem((2 * C, V), bf16),
            vmem((2 * C, V), bf16),
            vmem((2, ROWS, C), f32),
            vmem((8, C), f32),
            vmem((2, 8, PAD, C), f32),
            vmem((8, PAD, C), f32),
            vmem((8, PAD, C), f32),
            vmem((6, PAD, C), f32),
            vmem((6, 2, HALF, C), f32),
            vmem((6, QUART, C), f32),
            vmem((6, QUART, C), f32),
            vmem((2, HALF, C), f32),
            vmem((2, 2, HALF, C), f32),
            vmem((2, HALF, C), f32),
            vmem((2, HALF, C), f32),
            vmem((2, 2, HALF, C), f32),
            vmem((16, C), f32),
            vmem((16, 16, C), f32),
            dma((4,)),
            dma((3, 11)),
            dma((3, 11)),
            dma((2,)),
            dma((2,)),
            dma((4, 6)),
            dma((4, 6)),
            dma((2, 2)),
            dma((2, 2)),
            dma((3,)),
            dma((2,)),
            dma((16,)),
            dma((16,)),
        ],
        compiler_params=pltpu.CompilerParams(
            collective_id=0, has_side_effects=True, vmem_limit_bytes=56 * 1024 * 1024
        ),
        cost_estimate=pl.CostEstimate(
            flops=5 * 2 * V * ROWS * C, bytes_accessed=6 * 2**20, transcendentals=2 * V * C
        ),
    )(video_in, first_filter, first_bias.reshape(1, C), second_filter, grad_output)
    grad_input, grad_first, grad_second, grad_bias = outs
    return grad_input, grad_first, grad_second, grad_bias.reshape(C)


def solution(mesh):
    placed = (P("ta", "ha", "wa", None), P(), P(), P(), P("ta", "ha", "wa", None))
    return jax.shard_map(
        per_device,
        mesh=mesh,
        in_specs=placed,
        out_specs=(P("ta", "ha", "wa", None), P("ta", None), P("ta", None), P()),
        check_vma=False,
    )
```

```python
import jax
import jax.numpy as jnp
from jax import lax
from jax.experimental import pallas as pl
from jax.experimental.pallas import tpu as pltpu
from jax.sharding import PartitionSpec as P

f32, bf16 = jnp.float32, jnp.bfloat16
MESH = pl.DeviceIdType.MESH
C = 128
T, H, W = 4, 8, 16
V = T * H * W
ROWS = 27 * C
OWN = ROWS // 16
PAD = OWN + 8
HALF = PAD // 2
QUART = HALF // 2
LEFT = 8
LIMIT = float(54 * C * C + C)


def split(value):
    high = value.astype(bf16)
    low = (value - high.astype(f32)).astype(bf16)
    return high, low


def mod(value, count):
    return lax.rem(value + 2 * count, count)


def rows8(start, size):
    return pl.ds(pl.multiple_of(start, 8), size)


def remote(src, dst, send, recv, device):
    return pltpu.make_async_remote_copy(
        src_ref=src, dst_ref=dst, send_sem=send, recv_sem=recv, device_id=device,
        device_id_type=MESH,
    )


def kernel(
    video, first, bias, second, cot,
    grad_input, grad_first, grad_second, grad_bias,
    w_f32, w_split, ext, cols, cols_ext, shifted, acc, pre_ref, act_t, grad_t,
    raw, bias8, pack, summed, line_recv, line, plane_recv, share, full,
    note, notes, note2, notes2,
    local_sem, halo_send, halo_recv, core_send, core_recv, line_send, line_rcv,
    plane_send, plane_rcv, ag_send, ag_recv, n_send, n_recv, n2_send, n2_recv,
):
    ta, ha, wa = lax.axis_index("ta"), lax.axis_index("ha"), lax.axis_index("wa")
    core = lax.rem(ta, 2)
    x_hi = lax.rem(ta // 2, 2)
    z = ta // 4
    y = wa
    other = 1 - ha

    own_at = (2, 0, 0)
    blocks = [
        pltpu.make_async_copy(
            src, ext.at[n, pl.ds(own_at[n], T), pl.ds(1, H), pl.ds(LEFT, W)], local_sem.at[n]
        )
        for n, src in enumerate((video, cot))
    ]
    loads = [
        pltpu.make_async_copy(src, w_f32.at[n], local_sem.at[2 + n])
        for n, src in enumerate((first, second))
    ]
    for copy in blocks + loads:
        copy.start()

    gap = 9 * ha
    for n in range(3):
        ext[n, :, pl.ds(gap, 1)] = jnp.zeros((T + 2, 1, 32, C), f32)
        cols_ext[n, :, :, pl.ds(gap, 1)] = jnp.zeros((2, T + 2, 1, 1, C), f32)

    barrier = pltpu.get_barrier_semaphore()
    x = 2 * x_hi + ha

    def place(px, py, pz, pc):
        return (4 * pz + 2 * (px // 2) + pc, lax.rem(px, 2), py)

    xs = [mod(x + step, 4) for step in range(4)]
    ys = [mod(y + step, 4) for step in range(4)]
    zs = [mod(z + step, 4) for step in range(4)]
    plane_xy = [(i, j) for i in range(4) for j in range(4) if i or j]
    greeted = [place(xs[i], ys[j], z, core) for i, j in plane_xy]
    greeted += [place(xs[i], y, zs[j], core) for i in range(4) for j in (1, 2, 3)]
    greeted += [place(x, y, zs[j], 1 - core) for j in range(4)]
    greeted.append((mod(ta + 2 * core - 1, 16), ha, wa))
    for dt in (-1, 1):
        for row in (ha, other):
            for dw in (-1, 0, 1):
                if not (row is ha and dw == 0):
                    greeted.append((mod(ta + dt, 16), row, mod(wa + dw, 4)))
    for device in greeted:
        pl.semaphore_signal(barrier, inc=1, device_id=device, device_id_type=MESH)

    halo_at = (0, 4, 4)
    edge_at = (2, 0, 0)
    along = (1, -1, -1)
    edge_row = 7 * other

    def halo_plain(n, src):
        copies = []
        for slot, (dt, dh) in enumerate(((0, 1), (1, 0), (1, 1))):
            frames = pl.ds(edge_at[n], 2) if dt else pl.ds(0, T)
            to = pl.ds(halo_at[n], 2) if dt else pl.ds(own_at[n], T)
            rows = pl.ds(edge_row, 1) if dh else pl.ds(0, H)
            to_rows = pl.ds(gap, 1) if dh else pl.ds(1, H)
            copies.append(
                remote(
                    src(frames, rows),
                    ext.at[n, to, to_rows, pl.ds(LEFT, W)],
                    halo_send.at[n, slot], halo_recv.at[n, slot],
                    (mod(ta + along[n] * dt, 16), other if dh else ha, wa),
                )
            )
        return copies

    def halo_columns(n):
        copies = []
        slot = 3
        for dt in (0, 1):
            for dh in (0, 1):
                for side, dw in ((0, -1), (1, 1)):
                    if dt + dh + abs(dw) == 0:
                        continue
                    frames = pl.ds(edge_at[n], 2) if dt else pl.ds(0, T)
                    to = pl.ds(halo_at[n], 2) if dt else pl.ds(own_at[n], T)
                    rows = pl.ds(edge_row, 1) if dh else pl.ds(0, H)
                    to_rows = pl.ds(gap, 1) if dh else pl.ds(1, H)
                    copies.append(
                        remote(
                            cols.at[n, side, frames, rows],
                            cols_ext.at[n, 1 - side, to, to_rows],
                            halo_send.at[n, slot], halo_recv.at[n, slot],
                            (mod(ta + along[n] * dt, 16), other if dh else ha, mod(wa + dw, 4)),
                        )
                    )
                    slot += 1
        return copies

    def pack_columns(n):
        own = ext[n, pl.ds(own_at[n], T), pl.ds(1, H), pl.ds(LEFT, W)]
        cols[n, 0] = own[:, :, 0:1]
        cols[n, 1] = own[:, :, W - 1 : W]

    plain = [halo_plain(0, lambda t, h: video.at[t, h]), halo_plain(1, lambda t, h: cot.at[t, h])]
    strips = [halo_columns(0), halo_columns(1)]
    for n in (0, 1):
        blocks[n].wait()
        pack_columns(n)

    for copy in loads:
        copy.wait()

    def split_filters(tap, _):
        for n in range(2):
            high, low = split(w_f32[n, tap])
            w_split[n, tap, :, :C] = high
            w_split[n, tap, :, C:] = low
        return 0

    lax.fori_loop(0, 27, split_filters, 0)

    pl.semaphore_wait(barrier, len(greeted))
    for n in (0, 1):
        for copy in plain[n] + strips[n]:
            copy.start()

    def transposed(value, ref):
        high, low = split(value.T)
        ref[:C] = high
        ref[C:] = low

    left_in = (wa > 0).astype(f32)
    right_in = (wa < 3).astype(f32)
    frame_in = ((ta > 0).astype(f32), (ta < 15).astype(f32), (ta < 15).astype(f32))

    def shift_columns(n):
        def frame(t, _):
            ext[n, t, :, LEFT - 1 : LEFT] = cols_ext[n, 0, t] * left_in
            ext[n, t, :, LEFT + W : LEFT + W + 1] = cols_ext[n, 1, t] * right_in
            is_halo = jnp.logical_and(t >= halo_at[n], t < halo_at[n] + 2)
            keep = jnp.where(is_halo, frame_in[n], 1.0)
            for c in range(3):
                high, low = split(ext[n, t, :, LEFT - 1 + c : LEFT - 1 + c + W] * keep)
                shifted[n, c, t, :, :, :C] = high
                shifted[n, c, t, :, :, C:] = low
            return 0

        lax.fori_loop(0, T + 2, frame, 0)

    def conv(n, filters, back):
        for a in range(3):
            pieces, blocks_w = [], []
            for b in range(3):
                for c in range(3):
                    at = (2 - a, 2 - b, 2 - c) if back else (a, b, c)
                    window = shifted[n, at[2], pl.ds(at[0], T), pl.ds(at[1], H)]
                    pieces.append(window.reshape(V, 2 * C))
                    w = w_split[filters, 9 * a + 3 * b + c]
                    if back:
                        high, low = w[:, :C], w[:, C:]
                        blocks_w.append(
                            jnp.concatenate(
                                [
                                    jnp.concatenate([high, high], axis=1),
                                    jnp.concatenate([low, low], axis=1),
                                ],
                                axis=0,
                            )
                        )
                    else:
                        blocks_w += [w, w]
            columns = jnp.concatenate(pieces, axis=1)
            if back:
                product = lax.dot_general(
                    columns, jnp.concatenate(blocks_w, axis=1), (((1,), (1,)), ((), ())),
                    preferred_element_type=f32,
                )
            else:
                product = jnp.dot(
                    columns, jnp.concatenate(blocks_w, axis=0), preferred_element_type=f32
                )
            if a == 0:
                acc[...] = product
            else:
                acc[...] += product
        return acc[:, :C] + acc[:, C:]

    def weight_grad(fixed, n, f):
        def taps(step, _):
            p, q = step // 3, lax.rem(step, 3)
            for c in range(3):
                at = (p, q, c) if f else (2 - p, 2 - q, 2 - c)
                window = shifted[n, at[2], pl.ds(at[0], T), pl.ds(at[1], H)].reshape(V, 2 * C)
                o = jnp.dot(fixed[...], window, preferred_element_type=f32)
                o = (o[:C, :C] + o[C:, :C]) + (o[:C, C:] + o[C:, C:])
                raw[f, rows8((3 * step + c) * C, C)] = o.T if f else o
            return 0

        lax.fori_loop(0, 9, taps, 0)

    pieces = ((0, HALF), (HALF, QUART), (HALF + QUART, QUART - 8))

    def slots(kz, kx):
        return (
            (0, kz, kx * HALF),
            (1, 2 * kx, kz * QUART),
            (1, 2 * kx + 1, kz * QUART),
        )

    owners = [(kz, kx) for kz in range(4) for kx in range(2)]

    def core_swap(f):
        for kz, kx in owners:
            k = 4 * kz + 2 * kx + 1 - core
            for (start, size), (part, shard, to) in zip(pieces, slots(kz, kx)):
                pack[f, part, shard, to : to + size] = raw[f, rows8(OWN * k + start, size)]
            tail = kz * QUART + QUART - 8
            pack[f, 1, 2 * kx + 1, tail : tail + 8] = bias8[...] if f else jnp.zeros((8, C), f32)
        copy = remote(
            pack.at[f], summed.at[f], core_send.at[f], core_recv.at[f],
            (ta + 1 - 2 * core, ha, wa),
        )
        copy.start()
        return copy

    def core_add(f):
        for kz, kx in owners:
            k = 4 * kz + 2 * kx + core
            for (start, size), (part, shard, to) in zip(pieces, slots(kz, kx)):
                summed[f, part, shard, to : to + size] += raw[f, rows8(OWN * k + start, size)]
            if f:
                tail = kz * QUART + QUART - 8
                summed[f, 1, 2 * kx + 1, tail : tail + 8] += bias8[...]

    def line_start(f):
        copies = []
        for step in (1, 2, 3):
            for part, shard, device in (
                (0, zs[step], place(x, y, zs[step], core)),
                (1, ys[step], place(x, ys[step], z, core)),
            ):
                copies.append(
                    remote(
                        summed.at[f, part, shard], line_recv.at[f, part, step - 1],
                        line_send.at[f, part, step - 1], line_rcv.at[f, part, step - 1], device,
                    )
                )
        for copy in copies:
            copy.start()
        return copies

    def line_end(f, copies):
        for copy in copies:
            copy.wait_recv()
        for part, own in ((0, z), (1, y)):
            line[f, part] = (summed[f, part, own] + line_recv[f, part, 0]) + (
                line_recv[f, part, 1] + line_recv[f, part, 2]
            )

    def piece(part, px, other_axis):
        if part == 0:
            slot = 4 * lax.rem(other_axis, 2) + px
            return (other_axis // 2) * HALF + 16 * jnp.minimum(slot, 6)
        return other_axis * QUART + jnp.minimum(16 * px, 40)

    across = (y, z)

    def plane_copies(f):
        copies = []
        for part in (0, 1):
            mine = 4 * x + across[part]
            for n, (i, j) in enumerate(plane_xy):
                to = (ys, zs)[part][j]
                device = place(xs[i], to, z, core) if part == 0 else place(xs[i], y, to, core)
                copies.append(
                    remote(
                        line.at[f, part, rows8(piece(part, xs[i], to), 16)],
                        plane_recv.at[f, part, mine],
                        plane_send.at[f, part, n], plane_rcv.at[f, part, mine], device,
                    )
                )
        return copies

    def plane_start(f):
        copies = plane_copies(f)
        for copy in copies:
            copy.start()
        for part in (0, 1):
            plane_recv[f, part, 4 * x + across[part]] = line[
                f, part, rows8(piece(part, x, across[part]), 16)
            ]
        return copies

    def plane_end(f):
        for part in (0, 1):
            for n, (i, j) in enumerate(plane_xy):
                source = (ys, zs)[part][j]
                slot = 4 * xs[i] + source
                device = (
                    place(xs[i], source, z, core) if part == 0 else place(xs[i], y, source, core)
                )
                remote(
                    line.at[f, part, pl.ds(0, 16)], plane_recv.at[f, part, slot],
                    plane_send.at[f, part, n], plane_rcv.at[f, part, slot], device,
                ).wait_recv()
            share[f, part] = jnp.sum(plane_recv[f, part], axis=0)

    for copy in plain[0] + strips[0]:
        copy.wait_recv()
    shift_columns(0)
    pre = conv(0, 0, False) + bias[...]
    pre_ref[...] = pre
    sig = 1.0 / (1.0 + jnp.exp(-pre))
    transposed(pre * sig, act_t)

    for copy in plain[1] + strips[1]:
        copy.wait_recv()
    shift_columns(1)
    weight_grad(act_t, 1, 0)
    swap0 = core_swap(0)

    grad_act = conv(1, 1, True)
    pre = pre_ref[...]
    sig = 1.0 / (1.0 + jnp.exp(-pre))
    grad_pre = grad_act * sig * (1.0 + pre * (1.0 - sig))
    bias8[...] = jnp.sum(grad_pre.reshape(V // 8, 8, C), axis=0)
    ext[2, pl.ds(0, T), pl.ds(1, H), pl.ds(LEFT, W)] = grad_pre.reshape(T, H, W, C)
    transposed(grad_pre, grad_t)

    swap0.wait_recv()
    core_add(0)
    line0 = line_start(0)

    plain.append(
        halo_plain(2, lambda t, h: ext.at[2, t, pl.ds(h.start + 1, h.size), pl.ds(LEFT, W)])
    )
    pack_columns(2)
    strips.append(halo_columns(2))
    for copy in plain[2] + strips[2]:
        copy.start()

    weight_grad(grad_t, 0, 1)
    swap1 = core_swap(1)
    swap1.wait_recv()
    core_add(1)
    line1 = line_start(1)

    line_end(0, line0)
    plane0 = plane_start(0)

    for copy in plain[2] + strips[2]:
        copy.wait_recv()
    shift_columns(2)
    grad_input[...] = conv(2, 0, True).reshape(T, H, W, C)

    line_end(1, line1)
    plane1 = plane_start(1)
    plane_end(0)
    plane_end(1)

    last = x == 3
    odd = lax.rem(y, 2) == 1
    keep_low = jnp.where(jnp.logical_and(last, odd), 0.0, 1.0)
    keep_first = jnp.where(last, 0.0, 1.0)
    squares = jnp.zeros((8, C), f32)
    for f in range(2):
        squares += keep_low * (
            share[f, 0, :8] * share[f, 0, :8] + share[f, 0, 8:] * share[f, 0, 8:]
        )
        squares += keep_first * (share[f, 1, :8] * share[f, 1, :8])
        squares += keep_low * (share[f, 1, 8:] * share[f, 1, 8:])
    note[:8] = squares
    note[8:] = share[1, 1, 8:]
    here = 4 * x + y
    notes[here] = note[...]

    def tell(n, i, j, slot):
        return remote(
            note, notes.at[slot], n_send.at[n], n_recv.at[slot], place(xs[i], ys[j], z, core)
        )

    for n, (i, j) in enumerate(plane_xy):
        tell(n, i, j, here).start()

    wide = y // 2
    half_slot = 4 * lax.rem(y, 2) + x

    def give(i, j):
        return remote(
            share, full.at[half_slot], ag_send.at[4 * i + j], ag_recv.at[half_slot],
            place(2 * wide + i, ys[j], z, core),
        )

    def each_give(act_on):
        for i in range(2):

            @pl.when(2 * wide + i != x)
            def _(i=i):
                act_on(give(i, 0))

            for j in (1, 2, 3):
                act_on(give(i, j))

    each_give(lambda copy: copy.start())

    @pl.when(wide == x_hi)
    def _():
        full[half_slot] = share[...]

    for n, (i, j) in enumerate(plane_xy):
        tell(n, i, j, 4 * xs[i] + ys[j]).wait_recv()
    note2[:8] = jnp.sum(notes[:, :8], axis=0)
    note2[8:] = notes[13, 8:]
    there = 2 * z + core
    notes2[there] = note2[...]
    line_zc = [(j, c) for j in range(4) for c in range(2) if j or c]

    def tell2(n, j, c, slot):
        to_core = 1 - core if c else core
        return remote(
            note2, notes2.at[slot], n2_send.at[n], n2_recv.at[slot], place(x, y, zs[j], to_core)
        )

    for n, (j, c) in enumerate(line_zc):
        tell2(n, j, c, there).start()

    for part in range(2):
        for i in range(4):

            @pl.when(jnp.logical_or(x != i, y != 2 * x_hi + part))
            def _(part=part, i=i):
                slot = 4 * part + i
                remote(
                    share, full.at[slot], ag_send.at[0], ag_recv.at[slot],
                    place(x, ys[1], z, core),
                ).wait_recv()

    for n, (j, c) in enumerate(line_zc):
        tell2(n, j, c, 2 * zs[j] + (1 - core if c else core)).wait_recv()
    everything = jnp.sum(notes2[:, :8], axis=0)
    raw_bias = jnp.sum(notes2[0, 8:], axis=0, keepdims=True)
    norm2 = jnp.sum(everything, axis=(0, 1), keepdims=True) + jnp.sum(
        raw_bias * raw_bias, axis=(0, 1), keepdims=True
    )
    factor = jnp.minimum(1.0, jnp.sqrt(jnp.full((1, 1), LIMIT, f32)) / jnp.sqrt(norm2))
    for f, out in ((0, grad_second), (1, grad_first)):
        for slot in range(8):
            low = 16 * min(slot, 6)
            out[low : low + 16] = full[slot, f, 0] * factor
            high = HALF + QUART * (slot // 4) + min(16 * (slot % 4), 40)
            size = min(16, OWN - high)
            out[high : high + size] = full[slot, f, 1, :size] * factor
    grad_bias[...] = raw_bias * factor

    for copies in plain + strips + [[swap0, swap1], line0, line1, plane0, plane1]:
        for copy in copies:
            copy.wait_send()
    for n, (i, j) in enumerate(plane_xy):
        tell(n, i, j, here).wait_send()
    each_give(lambda copy: copy.wait_send())
    for n, (j, c) in enumerate(line_zc):
        tell2(n, j, c, there).wait_send()


def hand_over(*refs):
    for source, out in zip(refs[:4], refs[4:]):
        out[...] = source[...]


def per_device(video_in, first_filter, first_bias, second_filter, grad_output):
    vmem = pltpu.VMEM
    dma = pltpu.SemaphoreType.DMA
    any_spec = pl.BlockSpec(memory_space=pl.ANY)
    vmem_spec = pl.BlockSpec(memory_space=pltpu.VMEM)
    shapes = (
        jax.ShapeDtypeStruct((T, H, W, C), f32),
        jax.ShapeDtypeStruct((OWN, C), f32),
        jax.ShapeDtypeStruct((OWN, C), f32),
        jax.ShapeDtypeStruct((1, C), f32),
    )
    outs = pl.pallas_call(
        kernel,
        out_shape=shapes,
        in_specs=[any_spec, any_spec, vmem_spec, any_spec, any_spec],
        out_specs=[vmem_spec] * 4,
        scratch_shapes=[
            vmem((2, 27, C, C), f32),
            vmem((2, 27, C, 2 * C), bf16),
            vmem((3, T + 2, H + 2, 32, C), f32),
            vmem((3, 2, T, H, 1, C), f32),
            vmem((3, 2, T + 2, H + 2, 1, C), f32),
            vmem((3, 3, T + 2, H + 2, W, 2 * C), bf16),
            vmem((V, 2 * C), f32),
            vmem((V, C), f32),
            vmem((2 * C, V), bf16),
            vmem((2 * C, V), bf16),
            vmem((2, ROWS, C), f32),
            vmem((8, C), f32),
            vmem((2, 2, 4, PAD, C), f32),
            vmem((2, 2, 4, PAD, C), f32),
            vmem((2, 2, 3, PAD, C), f32),
            vmem((2, 2, PAD, C), f32),
            vmem((2, 2, 16, 16, C), f32),
            vmem((2, 2, 16, C), f32),
            vmem((8, 2, 2, 16, C), f32),
            vmem((16, C), f32),
            vmem((16, 16, C), f32),
            vmem((16, C), f32),
            vmem((8, 16, C), f32),
            dma((4,)),
            dma((3, 11)),
            dma((3, 11)),
            dma((2,)),
            dma((2,)),
            dma((2, 2, 3)),
            dma((2, 2, 3)),
            dma((2, 2, 15)),
            dma((2, 2, 16)),
            dma((8,)),
            dma((8,)),
            dma((15,)),
            dma((16,)),
            dma((7,)),
            dma((8,)),
        ],
        compiler_params=pltpu.CompilerParams(
            collective_id=0, has_side_effects=True, vmem_limit_bytes=56 * 1024 * 1024
        ),
        cost_estimate=pl.CostEstimate(
            flops=5 * 2 * V * ROWS * C, bytes_accessed=6 * 2**20, transcendentals=2 * V * C
        ),
    )(video_in, first_filter, first_bias.reshape(1, C), second_filter, grad_output)
    outs = pl.pallas_call(
        hand_over, out_shape=shapes, in_specs=[vmem_spec] * 4, out_specs=[vmem_spec] * 4
    )(*outs)
    grad_input, grad_first, grad_second, grad_bias = outs
    return grad_input, grad_first, grad_second, grad_bias.reshape(C)


def solution(mesh):
    placed = (P("ta", "ha", "wa", None), P(), P(), P(), P("ta", "ha", "wa", None))
    return jax.shard_map(
        per_device,
        mesh=mesh,
        in_specs=placed,
        out_specs=(P("ta", "ha", "wa", None), P("ta", None), P("ta", None), P()),
        check_vma=False,
    )
```

```python
import jax
import jax.numpy as jnp
from jax import lax
from jax.experimental import pallas as pl
from jax.experimental.pallas import tpu as pltpu
from jax.sharding import PartitionSpec as P

f32, bf16 = jnp.float32, jnp.bfloat16
MESH = pl.DeviceIdType.MESH
C = 128
T, H, W = 4, 8, 16
V = T * H * W
ROWS = 27 * C
OWN = ROWS // 16
PAD = OWN + 8
HALF = PAD // 2
QUART = HALF // 2
LEFT = 8
LIMIT = float(54 * C * C + C)


def split(value):
    high = value.astype(bf16)
    low = (value - high.astype(f32)).astype(bf16)
    return high, low


def mod(value, count):
    return lax.rem(value + 2 * count, count)


def rows8(start, size):
    return pl.ds(pl.multiple_of(start, 8), size)


def remote(src, dst, send, recv, device):
    return pltpu.make_async_remote_copy(
        src_ref=src, dst_ref=dst, send_sem=send, recv_sem=recv, device_id=device,
        device_id_type=MESH,
    )


def kernel(
    video, first, bias, second, cot,
    grad_input, grad_first, grad_second, grad_bias,
    w_f32, w_split, ext, cols, cols_ext, shifted, acc, pre_ref, act_t, grad_t,
    raw, bias8, pack, summed, line_recv, line, plane_recv, share, full,
    note, notes, note2, notes2,
    local_sem, halo_send, halo_recv, core_send, core_recv, line_send, line_rcv,
    plane_send, plane_rcv, ag_send, ag_recv, n_send, n_recv,
):
    ta, ha, wa = lax.axis_index("ta"), lax.axis_index("ha"), lax.axis_index("wa")
    core = lax.rem(ta, 2)
    x_hi = lax.rem(ta // 2, 2)
    z = ta // 4
    y = wa
    other = 1 - ha

    own_at = (2, 0, 0)
    blocks = [
        pltpu.make_async_copy(
            src, ext.at[n, pl.ds(own_at[n], T), pl.ds(1, H), pl.ds(LEFT, W)], local_sem.at[n]
        )
        for n, src in enumerate((video, cot))
    ]
    loads = [
        pltpu.make_async_copy(src, w_f32.at[n], local_sem.at[2 + n])
        for n, src in enumerate((first, second))
    ]
    for copy in blocks + loads:
        copy.start()

    gap = 9 * ha
    for n in range(3):
        ext[n, :, pl.ds(gap, 1)] = jnp.zeros((T + 2, 1, 32, C), f32)
        cols_ext[n, :, :, pl.ds(gap, 1)] = jnp.zeros((2, T + 2, 1, 1, C), f32)

    barrier = pltpu.get_barrier_semaphore()
    x = 2 * x_hi + ha

    def place(px, py, pz, pc):
        return (4 * pz + 2 * (px // 2) + pc, lax.rem(px, 2), py)

    xs = [mod(x + step, 4) for step in range(4)]
    ys = [mod(y + step, 4) for step in range(4)]
    zs = [mod(z + step, 4) for step in range(4)]
    hops = (0, 1, 2, 1)
    plane_xy = [(i, j) for i in range(4) for j in range(4) if i or j]
    plane_xy.sort(key=lambda at: -hops[at[0]] - hops[at[1]])

    def take(view, sem):
        pltpu.make_async_copy(view, view, sem).wait()

    greeted = []
    for dt in (-1, 1):
        for row in (other, ha):
            for dw in (-1, 1, 0):
                greeted.append((mod(ta + dt, 16), row, mod(wa + dw, 4)))
    greeted += [place(x, y, zs[j], core) for j in (2, 1, 3)]
    greeted += [(ta, other, mod(wa + dw, 4)) for dw in (-1, 1, 0)]
    greeted += [(ta, ha, mod(wa + dw, 4)) for dw in (-1, 1)]
    for device in greeted:
        pl.semaphore_signal(barrier, inc=1, device_id=device, device_id_type=MESH)

    halo_at = (0, 4, 4)
    edge_at = (2, 0, 0)
    along = (1, -1, -1)
    edge_row = 7 * other

    def halo_plain(n, src):
        copies = []
        for dt, dh in ((1, 1), (1, 0), (0, 1)):
            frames = pl.ds(edge_at[n], 2) if dt else pl.ds(0, T)
            to = pl.ds(halo_at[n], 2) if dt else pl.ds(own_at[n], T)
            rows = pl.ds(edge_row, 1) if dh else pl.ds(0, H)
            to_rows = pl.ds(gap, 1) if dh else pl.ds(1, H)
            copies.append(
                remote(
                    src(frames, rows),
                    ext.at[n, to, to_rows, pl.ds(LEFT, W)],
                    halo_send.at[n, 0], halo_recv.at[n, 0],
                    (mod(ta + along[n] * dt, 16), other if dh else ha, wa),
                )
            )
        return copies

    def halo_columns(n):
        copies = []
        for dt in (1, 0):
            for dh in (1, 0):
                for side, dw in ((0, -1), (1, 1)):
                    frames = pl.ds(edge_at[n], 2) if dt else pl.ds(0, T)
                    to = pl.ds(halo_at[n], 2) if dt else pl.ds(own_at[n], T)
                    rows = pl.ds(edge_row, 1) if dh else pl.ds(0, H)
                    to_rows = pl.ds(gap, 1) if dh else pl.ds(1, H)
                    copies.append(
                        remote(
                            cols.at[n, side, frames, rows],
                            cols_ext.at[n, 1 - side, to, to_rows],
                            halo_send.at[n, 1], halo_recv.at[n, 1],
                            (mod(ta + along[n] * dt, 16), other if dh else ha, mod(wa + dw, 4)),
                        )
                    )
        return copies

    plain_rows = T * W + 2 * H * W + 2 * W

    def halo_take(n, sems):
        take(raw.at[0, pl.ds(0, plain_rows)], sems.at[n, 0])
        take(cols_ext.at[n, :, :, pl.ds(0, H + 1)], sems.at[n, 1])

    def pack_columns(n):
        own = ext[n, pl.ds(own_at[n], T), pl.ds(1, H), pl.ds(LEFT, W)]
        cols[n, 0] = own[:, :, 0:1]
        cols[n, 1] = own[:, :, W - 1 : W]

    plain = [halo_plain(0, lambda t, h: video.at[t, h]), halo_plain(1, lambda t, h: cot.at[t, h])]
    strips = [halo_columns(0), halo_columns(1)]
    for n in (0, 1):
        blocks[n].wait()
        pack_columns(n)

    for copy in loads:
        copy.wait()

    def split_filters(tap, _):
        for n in range(2):
            high, low = split(w_f32[n, tap])
            w_split[n, tap, :, :C] = high
            w_split[n, tap, :, C:] = low
        return 0

    lax.fori_loop(0, 27, split_filters, 0)

    pl.semaphore_wait(barrier, len(greeted))
    for n in (0, 1):
        for copy in strips[n] + plain[n]:
            copy.start()

    def transposed(value, ref):
        high, low = split(value.T)
        ref[:C] = high
        ref[C:] = low

    left_in = (wa > 0).astype(f32)
    right_in = (wa < 3).astype(f32)
    frame_in = ((ta > 0).astype(f32), (ta < 15).astype(f32), (ta < 15).astype(f32))

    def shift_columns(n):
        def frame(t, _):
            ext[n, t, :, LEFT - 1 : LEFT] = cols_ext[n, 0, t] * left_in
            ext[n, t, :, LEFT + W : LEFT + W + 1] = cols_ext[n, 1, t] * right_in
            is_halo = jnp.logical_and(t >= halo_at[n], t < halo_at[n] + 2)
            keep = jnp.where(is_halo, frame_in[n], 1.0)
            for c in range(3):
                high, low = split(ext[n, t, :, LEFT - 1 + c : LEFT - 1 + c + W] * keep)
                shifted[n, c, t, :, :, :C] = high
                shifted[n, c, t, :, :, C:] = low
            return 0

        lax.fori_loop(0, T + 2, frame, 0)

    def conv(n, filters, back):
        for a in range(3):
            pieces, blocks_w = [], []
            for b in range(3):
                for c in range(3):
                    at = (2 - a, 2 - b, 2 - c) if back else (a, b, c)
                    window = shifted[n, at[2], pl.ds(at[0], T), pl.ds(at[1], H)]
                    pieces.append(window.reshape(V, 2 * C))
                    w = w_split[filters, 9 * a + 3 * b + c]
                    if back:
                        high, low = w[:, :C], w[:, C:]
                        blocks_w.append(
                            jnp.concatenate(
                                [
                                    jnp.concatenate([high, high], axis=1),
                                    jnp.concatenate([low, low], axis=1),
                                ],
                                axis=0,
                            )
                        )
                    else:
                        blocks_w += [w, w]
            columns = jnp.concatenate(pieces, axis=1)
            if back:
                product = lax.dot_general(
                    columns, jnp.concatenate(blocks_w, axis=1), (((1,), (1,)), ((), ())),
                    preferred_element_type=f32,
                )
            else:
                product = jnp.dot(
                    columns, jnp.concatenate(blocks_w, axis=0), preferred_element_type=f32
                )
            if a == 0:
                acc[...] = product
            else:
                acc[...] += product
        return acc[:, :C] + acc[:, C:]

    def weight_grad(fixed, n, f):
        def taps(step, _):
            p, q = step // 3, lax.rem(step, 3)
            for c in range(3):
                at = (p, q, c) if f else (2 - p, 2 - q, 2 - c)
                window = shifted[n, at[2], pl.ds(at[0], T), pl.ds(at[1], H)].reshape(V, 2 * C)
                o = jnp.dot(fixed[...], window, preferred_element_type=f32)
                o = (o[:C, :C] + o[C:, :C]) + (o[:C, C:] + o[C:, C:])
                raw[f, rows8((3 * step + c) * C, C)] = o.T if f else o
            return 0

        lax.fori_loop(0, 9, taps, 0)

    pieces = ((0, HALF), (HALF, QUART), (HALF + QUART, QUART - 8))

    def slots(kz, kx):
        return (
            (0, kz, kx * HALF),
            (1, 2 * kx, kz * QUART),
            (1, 2 * kx + 1, kz * QUART),
        )

    owners = [(kz, kx) for kz in range(4) for kx in range(2)]

    def core_swap(f):
        for kz, kx in owners:
            k = 4 * kz + 2 * kx + 1 - core
            for (start, size), (part, shard, to) in zip(pieces, slots(kz, kx)):
                pack[f, part, shard, to : to + size] = raw[f, rows8(OWN * k + start, size)]
            tail = kz * QUART + QUART - 8
            pack[f, 1, 2 * kx + 1, tail : tail + 8] = bias8[...] if f else jnp.zeros((8, C), f32)
        copy = remote(
            pack.at[f], summed.at[f], core_send.at[f], core_recv.at[f],
            (ta + 1 - 2 * core, ha, wa),
        )
        copy.start()
        return copy

    def core_add(f):
        for kz, kx in owners:
            k = 4 * kz + 2 * kx + core
            for (start, size), (part, shard, to) in zip(pieces, slots(kz, kx)):
                summed[f, part, shard, to : to + size] += raw[f, rows8(OWN * k + start, size)]
            if f:
                tail = kz * QUART + QUART - 8
                summed[f, 1, 2 * kx + 1, tail : tail + 8] += bias8[...]

    def line_start(f):
        copies = []
        for step in (2, 1, 3):
            for part, shard, device in (
                (0, zs[step], place(x, y, zs[step], core)),
                (1, ys[step], place(x, ys[step], z, core)),
            ):
                copies.append(
                    remote(
                        summed.at[f, part, shard], line_recv.at[f, part, step - 1],
                        line_send.at[f], line_rcv.at[f], device,
                    )
                )
        for copy in copies:
            copy.start()

    def line_end(f):
        take(line_recv.at[f], line_rcv.at[f])
        for part, own in ((0, z), (1, y)):
            line[f, part] = (summed[f, part, own] + line_recv[f, part, 0]) + (
                line_recv[f, part, 1] + line_recv[f, part, 2]
            )

    def piece(part, px, other_axis):
        if part == 0:
            slot = 4 * lax.rem(other_axis, 2) + px
            return (other_axis // 2) * HALF + 16 * jnp.minimum(slot, 6)
        return other_axis * QUART + jnp.minimum(16 * px, 40)

    across = (y, z)

    def plane_start(f):
        copies = []
        for part in (0, 1):
            mine = 4 * x + across[part]
            for i, j in plane_xy:
                to = (ys, zs)[part][j]
                device = place(xs[i], to, z, core) if part == 0 else place(xs[i], y, to, core)
                copies.append(
                    remote(
                        line.at[f, part, rows8(piece(part, xs[i], to), 16)],
                        plane_recv.at[f, part, mine],
                        plane_send.at[f, part], plane_rcv.at[f, part], device,
                    )
                )
        for copy in copies:
            copy.start()
        for part in (0, 1):
            plane_recv[f, part, 4 * x + across[part]] = line[
                f, part, rows8(piece(part, x, across[part]), 16)
            ]

    def plane_end(f):
        for part in (0, 1):
            take(plane_recv.at[f, part, pl.ds(0, 15)], plane_rcv.at[f, part])
            share[f, part] = jnp.sum(plane_recv[f, part], axis=0)

    halo_take(0, halo_recv)
    shift_columns(0)
    pre = conv(0, 0, False) + bias[...]
    pre_ref[...] = pre
    sig = 1.0 / (1.0 + jnp.exp(-pre))
    transposed(pre * sig, act_t)

    halo_take(1, halo_recv)
    shift_columns(1)
    weight_grad(act_t, 1, 0)
    swap0 = core_swap(0)

    grad_act = conv(1, 1, True)
    pre = pre_ref[...]
    sig = 1.0 / (1.0 + jnp.exp(-pre))
    grad_pre = grad_act * sig * (1.0 + pre * (1.0 - sig))
    bias8[...] = jnp.sum(grad_pre.reshape(V // 8, 8, C), axis=0)
    ext[2, pl.ds(0, T), pl.ds(1, H), pl.ds(LEFT, W)] = grad_pre.reshape(T, H, W, C)
    transposed(grad_pre, grad_t)

    swap0.wait_recv()
    core_add(0)
    line_start(0)

    plain.append(
        halo_plain(2, lambda t, h: ext.at[2, t, pl.ds(h.start + 1, h.size), pl.ds(LEFT, W)])
    )
    pack_columns(2)
    strips.append(halo_columns(2))
    for copy in strips[2] + plain[2]:
        copy.start()

    weight_grad(grad_t, 0, 1)
    swap1 = core_swap(1)
    swap1.wait_recv()
    core_add(1)
    line_start(1)

    line_end(0)
    plane_start(0)

    halo_take(2, halo_recv)
    shift_columns(2)
    grad_input[...] = conv(2, 0, True).reshape(T, H, W, C)

    line_end(1)
    plane_start(1)

    for n in range(3):
        halo_take(n, halo_send)
    swap0.wait_send()
    swap1.wait_send()
    for f in range(2):
        take(line_recv.at[f], line_send.at[f])
    for part in range(2):
        take(plane_recv.at[0, part, pl.ds(0, 15)], plane_send.at[0, part])
    plane_end(0)
    plane_end(1)

    last = x == 3
    odd = lax.rem(y, 2) == 1
    keep_low = jnp.where(jnp.logical_and(last, odd), 0.0, 1.0)
    keep_first = jnp.where(last, 0.0, 1.0)
    squares = jnp.zeros((8, C), f32)
    for f in range(2):
        squares += keep_low * (
            share[f, 0, :8] * share[f, 0, :8] + share[f, 0, 8:] * share[f, 0, 8:]
        )
        squares += keep_first * (share[f, 1, :8] * share[f, 1, :8])
        squares += keep_low * (share[f, 1, 8:] * share[f, 1, 8:])
    note[0:1] = jnp.sum(squares, axis=0, keepdims=True)
    note[1:2] = jnp.sum(share[1, 1, 8:], axis=0, keepdims=True)
    here = 4 * x + y
    notes[here] = note[...]

    for i, j in plane_xy:
        remote(
            note, notes.at[here], n_send.at[0], n_recv.at[0], place(xs[i], ys[j], z, core)
        ).start()

    wide = y // 2
    half_slot = 4 * lax.rem(y, 2) + x

    def give(i, j):
        return remote(
            share, full.at[half_slot], ag_send.at[0], ag_recv.at[0],
            place(2 * wide + i, ys[j], z, core),
        )

    for j in (2, 1, 3, 0):
        for i in range(2):
            if j:
                give(i, j).start()
            else:

                @pl.when(2 * wide + i != x)
                def _(i=i):
                    give(i, 0).start()

    @pl.when(wide == x_hi)
    def _():
        full[half_slot] = share[...]

    take(notes.at[pl.ds(0, 15)], n_recv.at[0])
    note2[0:1] = jnp.sum(notes[:, 0:1], axis=0)
    note2[1:2] = notes[13, 1:2]
    there = 2 * z + core
    notes2[there] = note2[...]
    for j, c in ((2, 1), (2, 0), (1, 1), (3, 1), (1, 0), (3, 0), (0, 1)):
        remote(
            note2, notes2.at[there], n_send.at[1], n_recv.at[1],
            place(x, y, zs[j], 1 - core if c else core),
        ).start()

    def shares_take(sem):
        @pl.when(wide == x_hi)
        def _():
            take(full.at[pl.ds(0, 7)], sem)

        @pl.when(wide != x_hi)
        def _():
            take(full, sem)

    shares_take(ag_recv.at[0])
    shares_take(ag_send.at[0])
    for part in range(2):
        take(plane_recv.at[1, part, pl.ds(0, 15)], plane_send.at[1, part])
    take(notes.at[pl.ds(0, 15)], n_send.at[0])

    take(notes2.at[pl.ds(0, 7)], n_recv.at[1])
    everything = jnp.sum(notes2[:, 0:1], axis=0)
    raw_bias = notes2[0, 1:2]
    norm2 = jnp.sum(everything, axis=(0, 1), keepdims=True) + jnp.sum(
        raw_bias * raw_bias, axis=(0, 1), keepdims=True
    )
    factor = jnp.minimum(1.0, jnp.sqrt(jnp.full((1, 1), LIMIT, f32)) / jnp.sqrt(norm2))
    for f, out in ((0, grad_second), (1, grad_first)):
        for slot in range(8):
            low = 16 * min(slot, 6)
            out[low : low + 16] = full[slot, f, 0] * factor
            high = HALF + QUART * (slot // 4) + min(16 * (slot % 4), 40)
            size = min(16, OWN - high)
            out[high : high + size] = full[slot, f, 1, :size] * factor
    grad_bias[...] = raw_bias * factor

    take(notes2.at[pl.ds(0, 7)], n_send.at[1])


def hand_over(*refs):
    for source, out in zip(refs[:4], refs[4:]):
        out[...] = source[...]


def per_device(video_in, first_filter, first_bias, second_filter, grad_output):
    vmem = pltpu.VMEM
    dma = pltpu.SemaphoreType.DMA
    any_spec = pl.BlockSpec(memory_space=pl.ANY)
    vmem_spec = pl.BlockSpec(memory_space=pltpu.VMEM)
    shapes = (
        jax.ShapeDtypeStruct((T, H, W, C), f32),
        jax.ShapeDtypeStruct((OWN, C), f32),
        jax.ShapeDtypeStruct((OWN, C), f32),
        jax.ShapeDtypeStruct((1, C), f32),
    )
    outs = pl.pallas_call(
        kernel,
        out_shape=shapes,
        in_specs=[any_spec, any_spec, vmem_spec, any_spec, any_spec],
        out_specs=[vmem_spec] * 4,
        scratch_shapes=[
            vmem((2, 27, C, C), f32),
            vmem((2, 27, C, 2 * C), bf16),
            vmem((3, T + 2, H + 2, 32, C), f32),
            vmem((3, 2, T, H, 1, C), f32),
            vmem((3, 2, T + 2, H + 2, 1, C), f32),
            vmem((3, 3, T + 2, H + 2, W, 2 * C), bf16),
            vmem((V, 2 * C), f32),
            vmem((V, C), f32),
            vmem((2 * C, V), bf16),
            vmem((2 * C, V), bf16),
            vmem((2, ROWS, C), f32),
            vmem((8, C), f32),
            vmem((2, 2, 4, PAD, C), f32),
            vmem((2, 2, 4, PAD, C), f32),
            vmem((2, 2, 3, PAD, C), f32),
            vmem((2, 2, PAD, C), f32),
            vmem((2, 2, 16, 16, C), f32),
            vmem((2, 2, 16, C), f32),
            vmem((8, 2, 2, 16, C), f32),
            vmem((2, C), f32),
            vmem((16, 2, C), f32),
            vmem((2, C), f32),
            vmem((8, 2, C), f32),
            dma((4,)),
            dma((3, 2)),
            dma((3, 2)),
            dma((2,)),
            dma((2,)),
            dma((2,)),
            dma((2,)),
            dma((2, 2)),
            dma((2, 2)),
            dma((1,)),
            dma((1,)),
            dma((2,)),
            dma((2,)),
        ],
        compiler_params=pltpu.CompilerParams(
            collective_id=0, has_side_effects=True, vmem_limit_bytes=56 * 1024 * 1024
        ),
        cost_estimate=pl.CostEstimate(
            flops=5 * 2 * V * ROWS * C, bytes_accessed=6 * 2**20, transcendentals=2 * V * C
        ),
    )(video_in, first_filter, first_bias.reshape(1, C), second_filter, grad_output)
    outs = pl.pallas_call(
        hand_over, out_shape=shapes, in_specs=[vmem_spec] * 4, out_specs=[vmem_spec] * 4
    )(*outs)
    grad_input, grad_first, grad_second, grad_bias = outs
    return grad_input, grad_first, grad_second, grad_bias.reshape(C)


def solution(mesh):
    placed = (P("ta", "ha", "wa", None), P(), P(), P(), P("ta", "ha", "wa", None))
    return jax.shard_map(
        per_device,
        mesh=mesh,
        in_specs=placed,
        out_specs=(P("ta", "ha", "wa", None), P("ta", None), P("ta", None), P()),
        check_vma=False,
    )
```

```python
import jax
import jax.numpy as jnp
from jax import lax
from jax.experimental import pallas as pl
from jax.experimental.pallas import tpu as pltpu
from jax.sharding import PartitionSpec as P

f32, bf16 = jnp.float32, jnp.bfloat16
MESH = pl.DeviceIdType.MESH
C = 128
T, H, W = 4, 8, 16
V = T * H * W
ROWS = 27 * C
OWN = ROWS // 16
PAD = OWN + 8
HALF = PAD // 2
QUART = HALF // 2
LEFT = 8
LIMIT = float(54 * C * C + C)


def split(value):
    high = value.astype(bf16)
    low = (value - high.astype(f32)).astype(bf16)
    return high, low


def mod(value, count):
    return lax.rem(value + 2 * count, count)


def rows8(start, size):
    return pl.ds(pl.multiple_of(start, 8), size)


def remote(src, dst, send, recv, device):
    return pltpu.make_async_remote_copy(
        src_ref=src, dst_ref=dst, send_sem=send, recv_sem=recv, device_id=device,
        device_id_type=MESH,
    )


def kernel(
    video, first, bias, second, cot,
    grad_input, grad_first, grad_second, grad_bias,
    w_f32, w_split, ext, cols, cols_ext, shifted, acc, pre_ref, act_t, grad_t,
    raw, bias8, pack, summed, line_recv, line, plane_recv, share, full,
    note, notes, note2, notes2, bias_v, gi_v, g_v, gb_v,
    local_sem, halo_send, halo_recv, core_send, core_recv, line_send, line_rcv,
    plane_send, plane_rcv, ag_send, ag_recv, n_send, n_recv,
):
    ta, ha, wa = lax.axis_index("ta"), lax.axis_index("ha"), lax.axis_index("wa")
    core = lax.rem(ta, 2)
    x_hi = lax.rem(ta // 2, 2)
    z = ta // 4
    y = wa
    other = 1 - ha

    barrier = pltpu.get_barrier_semaphore()
    x = 2 * x_hi + ha

    def place(px, py, pz, pc):
        return (4 * pz + 2 * (px // 2) + pc, lax.rem(px, 2), py)

    xs = [mod(x + step, 4) for step in range(4)]
    ys = [mod(y + step, 4) for step in range(4)]
    zs = [mod(z + step, 4) for step in range(4)]
    hops = (0, 1, 2, 1)
    plane_xy = [(i, j) for i in range(4) for j in range(4) if i or j]
    plane_xy.sort(key=lambda at: -hops[at[0]] - hops[at[1]])

    def take(view, sem):
        pltpu.make_async_copy(view, view, sem).wait()

    greeted = []
    for dt in (-1, 1):
        for row in (other, ha):
            for dw in (-1, 1, 0):
                greeted.append((mod(ta + dt, 16), row, mod(wa + dw, 4)))
    greeted += [place(x, y, zs[j], core) for j in (2, 1, 3)]
    greeted += [(ta, other, mod(wa + dw, 4)) for dw in (-1, 1, 0)]
    greeted += [(ta, ha, mod(wa + dw, 4)) for dw in (-1, 1)]
    for device in greeted:
        pl.semaphore_signal(barrier, inc=1, device_id=device, device_id_type=MESH)

    own_at = (2, 0, 0)
    blocks = [
        pltpu.make_async_copy(
            src, ext.at[n, pl.ds(own_at[n], T), pl.ds(1, H), pl.ds(LEFT, W)], local_sem.at[n]
        )
        for n, src in enumerate((video, cot))
    ]
    loads = [
        pltpu.make_async_copy(src, w_f32.at[n], local_sem.at[2 + n])
        for n, src in enumerate((first, second))
    ]
    bias_load = pltpu.make_async_copy(bias, bias_v, local_sem.at[4])
    for copy in blocks + [bias_load] + loads:
        copy.start()

    gap = 9 * ha
    for n in range(3):
        ext[n, :, pl.ds(gap, 1)] = jnp.zeros((T + 2, 1, 32, C), f32)
        cols_ext[n, :, :, pl.ds(gap, 1)] = jnp.zeros((2, T + 2, 1, 1, C), f32)

    halo_at = (0, 4, 4)
    edge_at = (2, 0, 0)
    along = (1, -1, -1)
    edge_row = 7 * other

    def halo_plain(n, src):
        copies = []
        for dt, dh in ((1, 1), (1, 0), (0, 1)):
            frames = pl.ds(edge_at[n], 2) if dt else pl.ds(0, T)
            to = pl.ds(halo_at[n], 2) if dt else pl.ds(own_at[n], T)
            rows = pl.ds(edge_row, 1) if dh else pl.ds(0, H)
            to_rows = pl.ds(gap, 1) if dh else pl.ds(1, H)
            copies.append(
                remote(
                    src(frames, rows),
                    ext.at[n, to, to_rows, pl.ds(LEFT, W)],
                    halo_send.at[n, 0], halo_recv.at[n, 0],
                    (mod(ta + along[n] * dt, 16), other if dh else ha, wa),
                )
            )
        return copies

    def halo_columns(n):
        copies = []
        for dt in (1, 0):
            for dh in (1, 0):
                for side, dw in ((0, -1), (1, 1)):
                    frames = pl.ds(edge_at[n], 2) if dt else pl.ds(0, T)
                    to = pl.ds(halo_at[n], 2) if dt else pl.ds(own_at[n], T)
                    rows = pl.ds(edge_row, 1) if dh else pl.ds(0, H)
                    to_rows = pl.ds(gap, 1) if dh else pl.ds(1, H)
                    copies.append(
                        remote(
                            cols.at[n, side, frames, rows],
                            cols_ext.at[n, 1 - side, to, to_rows],
                            halo_send.at[n, 1], halo_recv.at[n, 1],
                            (mod(ta + along[n] * dt, 16), other if dh else ha, mod(wa + dw, 4)),
                        )
                    )
        return copies

    plain_rows = T * W + 2 * H * W + 2 * W

    def halo_take(n, sems):
        take(raw.at[0, pl.ds(0, plain_rows)], sems.at[n, 0])
        take(cols_ext.at[n, :, :, pl.ds(0, H + 1)], sems.at[n, 1])

    def pack_columns(n):
        own = ext[n, pl.ds(own_at[n], T), pl.ds(1, H), pl.ds(LEFT, W)]
        cols[n, 0] = own[:, :, 0:1]
        cols[n, 1] = own[:, :, W - 1 : W]

    plain = [halo_plain(0, lambda t, h: video.at[t, h]), halo_plain(1, lambda t, h: cot.at[t, h])]
    strips = [halo_columns(0), halo_columns(1)]
    for n in (0, 1):
        blocks[n].wait()
        pack_columns(n)

    for copy in loads:
        copy.wait()
    bias_load.wait()

    def split_filters(tap, _):
        for n in range(2):
            high, low = split(w_f32[n, tap])
            w_split[n, tap, :, :C] = high
            w_split[n, tap, :, C:] = low
        return 0

    lax.fori_loop(0, 27, split_filters, 0)

    pl.semaphore_wait(barrier, len(greeted))
    for n in (0, 1):
        for copy in strips[n] + plain[n]:
            copy.start()

    def transposed(value, ref):
        high, low = split(value.T)
        ref[:C] = high
        ref[C:] = low

    left_in = (wa > 0).astype(f32)
    right_in = (wa < 3).astype(f32)
    frame_in = ((ta > 0).astype(f32), (ta < 15).astype(f32), (ta < 15).astype(f32))

    def shift_columns(n):
        def frame(t, _):
            ext[n, t, :, LEFT - 1 : LEFT] = cols_ext[n, 0, t] * left_in
            ext[n, t, :, LEFT + W : LEFT + W + 1] = cols_ext[n, 1, t] * right_in
            is_halo = jnp.logical_and(t >= halo_at[n], t < halo_at[n] + 2)
            keep = jnp.where(is_halo, frame_in[n], 1.0)
            for c in range(3):
                high, low = split(ext[n, t, :, LEFT - 1 + c : LEFT - 1 + c + W] * keep)
                shifted[n, c, t, :, :, :C] = high
                shifted[n, c, t, :, :, C:] = low
            return 0

        lax.fori_loop(0, T + 2, frame, 0)

    def conv(n, filters, back):
        for a in range(3):
            pieces, blocks_w = [], []
            for b in range(3):
                for c in range(3):
                    at = (2 - a, 2 - b, 2 - c) if back else (a, b, c)
                    window = shifted[n, at[2], pl.ds(at[0], T), pl.ds(at[1], H)]
                    pieces.append(window.reshape(V, 2 * C))
                    w = w_split[filters, 9 * a + 3 * b + c]
                    if back:
                        high, low = w[:, :C], w[:, C:]
                        blocks_w.append(
                            jnp.concatenate(
                                [
                                    jnp.concatenate([high, high], axis=1),
                                    jnp.concatenate([low, low], axis=1),
                                ],
                                axis=0,
                            )
                        )
                    else:
                        blocks_w += [w, w]
            columns = jnp.concatenate(pieces, axis=1)
            if back:
                product = lax.dot_general(
                    columns, jnp.concatenate(blocks_w, axis=1), (((1,), (1,)), ((), ())),
                    preferred_element_type=f32,
                )
            else:
                product = jnp.dot(
                    columns, jnp.concatenate(blocks_w, axis=0), preferred_element_type=f32
                )
            if a == 0:
                acc[...] = product
            else:
                acc[...] += product
        return acc[:, :C] + acc[:, C:]

    def weight_grad(fixed, n, f):
        def taps(p, _):
            for m in range(9):
                q, c = m // 3, m % 3
                at = (p, q, c) if f else (2 - p, 2 - q, 2 - c)
                window = shifted[n, at[2], pl.ds(at[0], T), pl.ds(at[1], H)].reshape(V, 2 * C)
                o = jnp.dot(fixed[...], window, preferred_element_type=f32)
                o = (o[:C, :C] + o[C:, :C]) + (o[:C, C:] + o[C:, C:])
                raw[f, rows8((9 * p + m) * C, C)] = o.T if f else o
            return 0

        lax.fori_loop(0, 3, taps, 0)

    pieces = ((0, HALF), (HALF, QUART), (HALF + QUART, QUART - 8))

    def slots(kz, kx):
        return (
            (0, kz, kx * HALF),
            (1, 2 * kx, kz * QUART),
            (1, 2 * kx + 1, kz * QUART),
        )

    owners = [(kz, kx) for kz in range(4) for kx in range(2)]

    def core_swap(f):
        for kz, kx in owners:
            k = 4 * kz + 2 * kx + 1 - core
            for (start, size), (part, shard, to) in zip(pieces, slots(kz, kx)):
                pack[f, part, shard, to : to + size] = raw[f, rows8(OWN * k + start, size)]
            tail = kz * QUART + QUART - 8
            pack[f, 1, 2 * kx + 1, tail : tail + 8] = bias8[...] if f else jnp.zeros((8, C), f32)
        copy = remote(
            pack.at[f], summed.at[f], core_send.at[f], core_recv.at[f],
            (ta + 1 - 2 * core, ha, wa),
        )
        copy.start()
        return copy

    def core_add(f):
        for kz, kx in owners:
            k = 4 * kz + 2 * kx + core
            for (start, size), (part, shard, to) in zip(pieces, slots(kz, kx)):
                summed[f, part, shard, to : to + size] += raw[f, rows8(OWN * k + start, size)]
            if f:
                tail = kz * QUART + QUART - 8
                summed[f, 1, 2 * kx + 1, tail : tail + 8] += bias8[...]

    def line_start(f):
        copies = []
        for step in (2, 1, 3):
            for part, shard, device in (
                (0, zs[step], place(x, y, zs[step], core)),
                (1, ys[step], place(x, ys[step], z, core)),
            ):
                copies.append(
                    remote(
                        summed.at[f, part, shard], line_recv.at[f, part, step - 1],
                        line_send.at[f], line_rcv.at[f], device,
                    )
                )
        for copy in copies:
            copy.start()

    def line_end(f):
        take(line_recv.at[f], line_rcv.at[f])
        for part, own in ((0, z), (1, y)):
            line[f, part] = (summed[f, part, own] + line_recv[f, part, 0]) + (
                line_recv[f, part, 1] + line_recv[f, part, 2]
            )

    def piece(part, px, other_axis):
        if part == 0:
            slot = 4 * lax.rem(other_axis, 2) + px
            return (other_axis // 2) * HALF + 16 * jnp.minimum(slot, 6)
        return other_axis * QUART + jnp.minimum(16 * px, 40)

    across = (y, z)

    def plane_start(f):
        copies, far = [], []
        for part in (0, 1):
            mine = 4 * x + across[part]
            for i, j in plane_xy:
                to = (ys, zs)[part][j]
                device = place(xs[i], to, z, core) if part == 0 else place(xs[i], y, to, core)
                far.append(-hops[i] - hops[j])
                copies.append(
                    remote(
                        line.at[f, part, rows8(piece(part, xs[i], to), 16)],
                        plane_recv.at[f, part, mine],
                        plane_send.at[f, part], plane_rcv.at[f, part], device,
                    )
                )
        for n in sorted(range(30), key=lambda n: far[n]):
            copies[n].start()
        for part in (0, 1):
            plane_recv[f, part, 4 * x + across[part]] = line[
                f, part, rows8(piece(part, x, across[part]), 16)
            ]

    def plane_end(f):
        for part in (0, 1):
            take(plane_recv.at[f, part, pl.ds(0, 15)], plane_rcv.at[f, part])
            share[f, part] = jnp.sum(plane_recv[f, part], axis=0)

    halo_take(0, halo_recv)
    shift_columns(0)
    pre = conv(0, 0, False) + bias_v[...]
    pre_ref[...] = pre
    sig = 1.0 / (1.0 + jnp.exp(-pre))
    transposed(pre * sig, act_t)

    halo_take(1, halo_recv)
    shift_columns(1)
    weight_grad(act_t, 1, 0)
    swap0 = core_swap(0)

    grad_act = conv(1, 1, True)
    pre = pre_ref[...]
    sig = 1.0 / (1.0 + jnp.exp(-pre))
    grad_pre = grad_act * sig * (1.0 + pre * (1.0 - sig))
    bias8[...] = jnp.sum(grad_pre.reshape(V // 8, 8, C), axis=0)
    ext[2, pl.ds(0, T), pl.ds(1, H), pl.ds(LEFT, W)] = grad_pre.reshape(T, H, W, C)
    transposed(grad_pre, grad_t)

    swap0.wait_recv()
    core_add(0)
    line_start(0)

    weight_grad(grad_t, 0, 1)
    swap1 = core_swap(1)
    swap1.wait_recv()
    core_add(1)
    line_start(1)

    plain.append(
        halo_plain(2, lambda t, h: ext.at[2, t, pl.ds(h.start + 1, h.size), pl.ds(LEFT, W)])
    )
    pack_columns(2)
    strips.append(halo_columns(2))
    for copy in strips[2] + plain[2]:
        copy.start()

    line_end(0)
    plane_start(0)

    def input_grad():
        gi_v[...] = conv(2, 0, True).reshape(T, H, W, C)
        gi_out.start()

    gi_out = pltpu.make_async_copy(gi_v, grad_input, local_sem.at[5])

    line_end(1)
    plane_start(1)

    for n in range(3):
        halo_take(n, halo_send)
    swap0.wait_send()
    swap1.wait_send()
    for f in range(2):
        take(line_recv.at[f], line_send.at[f])
    for part in range(2):
        take(plane_recv.at[0, part, pl.ds(0, 15)], plane_send.at[0, part])
    plane_end(0)
    halo_take(2, halo_recv)
    shift_columns(2)
    input_grad()
    plane_end(1)

    last = x == 3
    odd = lax.rem(y, 2) == 1
    keep_low = jnp.where(jnp.logical_and(last, odd), 0.0, 1.0)
    keep_first = jnp.where(last, 0.0, 1.0)
    squares = jnp.zeros((8, C), f32)
    for f in range(2):
        squares += keep_low * (
            share[f, 0, :8] * share[f, 0, :8] + share[f, 0, 8:] * share[f, 0, 8:]
        )
        squares += keep_first * (share[f, 1, :8] * share[f, 1, :8])
        squares += keep_low * (share[f, 1, 8:] * share[f, 1, 8:])
    note[0:1] = jnp.sum(squares, axis=0, keepdims=True)
    note[1:2] = jnp.sum(share[1, 1, 8:], axis=0, keepdims=True)
    here = 4 * x + y
    notes[here] = note[...]

    for i, j in plane_xy:
        remote(
            note, notes.at[here], n_send.at[0], n_recv.at[0], place(xs[i], ys[j], z, core)
        ).start()

    wide = y // 2
    half_slot = 4 * lax.rem(y, 2) + x

    def give(i, j):
        return remote(
            share, full.at[half_slot], ag_send.at[0], ag_recv.at[0],
            place(2 * wide + i, ys[j], z, core),
        )

    for j in (2, 1, 3, 0):
        for i in range(2):
            if j:
                give(i, j).start()
            else:

                @pl.when(2 * wide + i != x)
                def _(i=i):
                    give(i, 0).start()

    @pl.when(wide == x_hi)
    def _():
        full[half_slot] = share[...]

    take(notes.at[pl.ds(0, 15)], n_recv.at[0])
    note2[0:1] = jnp.sum(notes[:, 0:1], axis=0)
    note2[1:2] = notes[13, 1:2]
    there = 2 * z + core
    notes2[there] = note2[...]
    for j, c in ((2, 1), (2, 0), (1, 1), (3, 1), (1, 0), (3, 0), (0, 1)):
        remote(
            note2, notes2.at[there], n_send.at[1], n_recv.at[1],
            place(x, y, zs[j], 1 - core if c else core),
        ).start()

    def shares_take(sem):
        @pl.when(wide == x_hi)
        def _():
            take(full.at[pl.ds(0, 7)], sem)

        @pl.when(wide != x_hi)
        def _():
            take(full, sem)

    shares_take(ag_recv.at[0])
    shares_take(ag_send.at[0])
    for part in range(2):
        take(plane_recv.at[1, part, pl.ds(0, 15)], plane_send.at[1, part])
    take(notes.at[pl.ds(0, 15)], n_send.at[0])

    take(notes2.at[pl.ds(0, 7)], n_recv.at[1])
    everything = jnp.sum(notes2[:, 0:1], axis=0)
    raw_bias = notes2[0, 1:2]
    norm2 = jnp.sum(everything, axis=(0, 1), keepdims=True) + jnp.sum(
        raw_bias * raw_bias, axis=(0, 1), keepdims=True
    )
    factor = jnp.minimum(1.0, jnp.sqrt(jnp.full((1, 1), LIMIT, f32)) / jnp.sqrt(norm2))
    for f in range(2):
        out = g_v.at[f]
        for slot in range(8):
            low = 16 * min(slot, 6)
            out[low : low + 16] = full[slot, f, 0] * factor
            high = HALF + QUART * (slot // 4) + min(16 * (slot % 4), 40)
            size = min(16, OWN - high)
            out[high : high + size] = full[slot, f, 1, :size] * factor
    gb_v[...] = raw_bias * factor
    lasts = [
        pltpu.make_async_copy(src, dst, local_sem.at[n])
        for n, (src, dst) in enumerate(
            ((g_v.at[1], grad_first), (g_v.at[0], grad_second), (gb_v, grad_bias))
        )
    ]
    for copy in lasts:
        copy.start()
    for copy in lasts + [gi_out]:
        copy.wait()

    take(notes2.at[pl.ds(0, 7)], n_send.at[1])


def hand_over(*refs):
    for source, out in zip(refs[:4], refs[4:]):
        out[...] = source[...]


def per_device(video_in, first_filter, first_bias, second_filter, grad_output):
    vmem = pltpu.VMEM
    dma = pltpu.SemaphoreType.DMA
    any_spec = pl.BlockSpec(memory_space=pl.ANY)
    vmem_spec = pl.BlockSpec(memory_space=pltpu.VMEM)
    shapes = (
        jax.ShapeDtypeStruct((T, H, W, C), f32),
        jax.ShapeDtypeStruct((OWN, C), f32),
        jax.ShapeDtypeStruct((OWN, C), f32),
        jax.ShapeDtypeStruct((1, C), f32),
    )
    outs = pl.pallas_call(
        kernel,
        out_shape=shapes,
        in_specs=[any_spec] * 5,
        out_specs=[any_spec] * 4,
        scratch_shapes=[
            vmem((2, 27, C, C), f32),
            vmem((2, 27, C, 2 * C), bf16),
            vmem((3, T + 2, H + 2, 32, C), f32),
            vmem((3, 2, T, H, 1, C), f32),
            vmem((3, 2, T + 2, H + 2, 1, C), f32),
            vmem((3, 3, T + 2, H + 2, W, 2 * C), bf16),
            vmem((V, 2 * C), f32),
            vmem((V, C), f32),
            vmem((2 * C, V), bf16),
            vmem((2 * C, V), bf16),
            vmem((2, ROWS, C), f32),
            vmem((8, C), f32),
            vmem((2, 2, 4, PAD, C), f32),
            vmem((2, 2, 4, PAD, C), f32),
            vmem((2, 2, 3, PAD, C), f32),
            vmem((2, 2, PAD, C), f32),
            vmem((2, 2, 16, 16, C), f32),
            vmem((2, 2, 16, C), f32),
            vmem((8, 2, 2, 16, C), f32),
            vmem((2, C), f32),
            vmem((16, 2, C), f32),
            vmem((2, C), f32),
            vmem((8, 2, C), f32),
            vmem((1, C), f32),
            vmem((T, H, W, C), f32),
            vmem((2, OWN, C), f32),
            vmem((1, C), f32),
            dma((6,)),
            dma((3, 2)),
            dma((3, 2)),
            dma((2,)),
            dma((2,)),
            dma((2,)),
            dma((2,)),
            dma((2, 2)),
            dma((2, 2)),
            dma((1,)),
            dma((1,)),
            dma((2,)),
            dma((2,)),
        ],
        compiler_params=pltpu.CompilerParams(
            collective_id=0, has_side_effects=True, vmem_limit_bytes=56 * 1024 * 1024
        ),
        cost_estimate=pl.CostEstimate(
            flops=5 * 2 * V * ROWS * C, bytes_accessed=6 * 2**20, transcendentals=2 * V * C
        ),
    )(video_in, first_filter, first_bias.reshape(1, C), second_filter, grad_output)
    outs = pl.pallas_call(
        hand_over, out_shape=shapes, in_specs=[vmem_spec] * 4, out_specs=[vmem_spec] * 4
    )(*outs)
    grad_input, grad_first, grad_second, grad_bias = outs
    return grad_input, grad_first, grad_second, grad_bias.reshape(C)


def solution(mesh):
    placed = (P("ta", "ha", "wa", None), P(), P(), P(), P("ta", "ha", "wa", None))
    return jax.shard_map(
        per_device,
        mesh=mesh,
        in_specs=placed,
        out_specs=(P("ta", "ha", "wa", None), P("ta", None), P("ta", None), P()),
        check_vma=False,
    )
```

```python
import jax
import jax.numpy as jnp
from jax import lax
from jax.experimental import pallas as pl
from jax.experimental.pallas import tpu as pltpu
from jax.sharding import PartitionSpec as P

f32, bf16 = jnp.float32, jnp.bfloat16
MESH = pl.DeviceIdType.MESH
C = 128
T, H, W = 4, 8, 16
V = T * H * W
ROWS = 27 * C
OWN = ROWS // 16
PAD = OWN + 8
FIRST, SECOND, THIRD = 80, 40, 32
SHARD = (2 * FIRST, 4 * SECOND, 4 * THIRD)
LEFT = 8
LIMIT = float(54 * C * C + C)


def split(value):
    high = value.astype(bf16)
    low = (value - high.astype(f32)).astype(bf16)
    return high, low


def mod(value, count):
    return lax.rem(value + 2 * count, count)


def rows8(start, size):
    return pl.ds(pl.multiple_of(start, 8), size)


def remote(src, dst, send, recv, device):
    return pltpu.make_async_remote_copy(
        src_ref=src, dst_ref=dst, send_sem=send, recv_sem=recv, device_id=device,
        device_id_type=MESH,
    )


def kernel(
    video, first, bias, second, cot,
    grad_input, grad_first, grad_second, grad_bias,
    w_f32, w_split, ext, cols, cols_ext, shifted, acc, pre_ref, act_t, grad_t,
    raw, bias8, pack, summed, line_recv, line, plane_recv, share, full, third,
    note, notes, note2, notes2, bias_v, gi_v, g_v, gb_v,
    local_sem, halo_send, halo_recv, core_send, core_recv, line_send, line_rcv,
    plane_send, plane_rcv, ag_send, ag_recv, n_send, n_recv,
):
    ta, ha, wa = lax.axis_index("ta"), lax.axis_index("ha"), lax.axis_index("wa")
    core = lax.rem(ta, 2)
    x_hi = lax.rem(ta // 2, 2)
    z = ta // 4
    y = wa
    other = 1 - ha

    barrier = pltpu.get_barrier_semaphore()
    x = 2 * x_hi + ha

    def place(px, py, pz, pc):
        return (4 * pz + 2 * (px // 2) + pc, lax.rem(px, 2), py)

    xs = [mod(x + step, 4) for step in range(4)]
    ys = [mod(y + step, 4) for step in range(4)]
    zs = [mod(z + step, 4) for step in range(4)]
    hops = (0, 1, 2, 1)
    plane_xy = [(i, j) for i in range(4) for j in range(4) if i or j]
    plane_xy.sort(key=lambda at: -hops[at[0]] - hops[at[1]])

    def take(view, sem):
        pltpu.make_async_copy(view, view, sem).wait()

    greeted = []
    for dt in (-1, 1):
        for row in (other, ha):
            for dw in (-1, 1, 0):
                greeted.append((mod(ta + dt, 16), row, mod(wa + dw, 4)))
    greeted += [place(x, y, zs[j], core) for j in (2, 1, 3)]
    greeted += [(ta, other, mod(wa + dw, 4)) for dw in (-1, 1, 0)]
    greeted += [(ta, ha, mod(wa + dw, 4)) for dw in (-1, 1)]
    for device in greeted:
        pl.semaphore_signal(barrier, inc=1, device_id=device, device_id_type=MESH)

    own_at = (2, 0, 0)
    blocks = [
        pltpu.make_async_copy(
            src, ext.at[n, pl.ds(own_at[n], T), pl.ds(1, H), pl.ds(LEFT, W)], local_sem.at[n]
        )
        for n, src in enumerate((video, cot))
    ]
    loads = [
        pltpu.make_async_copy(src, w_f32.at[n], local_sem.at[2 + n])
        for n, src in enumerate((first, second))
    ]
    bias_load = pltpu.make_async_copy(bias, bias_v, local_sem.at[4])
    for copy in blocks + [bias_load] + loads:
        copy.start()

    gap = 9 * ha
    for n in range(3):
        ext[n, :, pl.ds(gap, 1)] = jnp.zeros((T + 2, 1, 32, C), f32)
        cols_ext[n, :, :, pl.ds(gap, 1)] = jnp.zeros((2, T + 2, 1, 1, C), f32)

    halo_at = (0, 4, 4)
    edge_at = (2, 0, 0)
    along = (1, -1, -1)
    edge_row = 7 * other

    def halo_plain(n, src):
        copies = []
        for dt, dh in ((1, 1), (1, 0), (0, 1)):
            frames = pl.ds(edge_at[n], 2) if dt else pl.ds(0, T)
            to = pl.ds(halo_at[n], 2) if dt else pl.ds(own_at[n], T)
            rows = pl.ds(edge_row, 1) if dh else pl.ds(0, H)
            to_rows = pl.ds(gap, 1) if dh else pl.ds(1, H)
            copies.append(
                remote(
                    src(frames, rows),
                    ext.at[n, to, to_rows, pl.ds(LEFT, W)],
                    halo_send.at[n, 0], halo_recv.at[n, 0],
                    (mod(ta + along[n] * dt, 16), other if dh else ha, wa),
                )
            )
        return copies

    def halo_columns(n):
        copies = []
        for dt in (1, 0):
            for dh in (1, 0):
                for side, dw in ((0, -1), (1, 1)):
                    frames = pl.ds(edge_at[n], 2) if dt else pl.ds(0, T)
                    to = pl.ds(halo_at[n], 2) if dt else pl.ds(own_at[n], T)
                    rows = pl.ds(edge_row, 1) if dh else pl.ds(0, H)
                    to_rows = pl.ds(gap, 1) if dh else pl.ds(1, H)
                    copies.append(
                        remote(
                            cols.at[n, side, frames, rows],
                            cols_ext.at[n, 1 - side, to, to_rows],
                            halo_send.at[n, 1], halo_recv.at[n, 1],
                            (mod(ta + along[n] * dt, 16), other if dh else ha, mod(wa + dw, 4)),
                        )
                    )
        return copies

    plain_rows = T * W + 2 * H * W + 2 * W

    def halo_take(n, sems):
        take(raw.at[0, pl.ds(0, plain_rows)], sems.at[n, 0])
        take(cols_ext.at[n, :, :, pl.ds(0, H + 1)], sems.at[n, 1])

    def pack_columns(n):
        own = ext[n, pl.ds(own_at[n], T), pl.ds(1, H), pl.ds(LEFT, W)]
        cols[n, 0] = own[:, :, 0:1]
        cols[n, 1] = own[:, :, W - 1 : W]

    plain = [halo_plain(0, lambda t, h: video.at[t, h]), halo_plain(1, lambda t, h: cot.at[t, h])]
    strips = [halo_columns(0), halo_columns(1)]
    for n in (0, 1):
        blocks[n].wait()
        pack_columns(n)

    for copy in loads:
        copy.wait()
    bias_load.wait()

    def split_filters(tap, _):
        for n in range(2):
            high, low = split(w_f32[n, tap])
            w_split[n, tap, :, :C] = high
            w_split[n, tap, :, C:] = low
        return 0

    lax.fori_loop(0, 27, split_filters, 0)

    pl.semaphore_wait(barrier, len(greeted))
    for n in (0, 1):
        for copy in strips[n] + plain[n]:
            copy.start()

    def transposed(value, ref):
        high, low = split(value.T)
        ref[:C] = high
        ref[C:] = low

    left_in = (wa > 0).astype(f32)
    right_in = (wa < 3).astype(f32)
    frame_in = ((ta > 0).astype(f32), (ta < 15).astype(f32), (ta < 15).astype(f32))

    def shift_columns(n):
        def frame(t, _):
            ext[n, t, :, LEFT - 1 : LEFT] = cols_ext[n, 0, t] * left_in
            ext[n, t, :, LEFT + W : LEFT + W + 1] = cols_ext[n, 1, t] * right_in
            is_halo = jnp.logical_and(t >= halo_at[n], t < halo_at[n] + 2)
            keep = jnp.where(is_halo, frame_in[n], 1.0)
            for c in range(3):
                high, low = split(ext[n, t, :, LEFT - 1 + c : LEFT - 1 + c + W] * keep)
                shifted[n, c, t, :, :, :C] = high
                shifted[n, c, t, :, :, C:] = low
            return 0

        lax.fori_loop(0, T + 2, frame, 0)

    def conv(n, filters, back):
        for a in range(3):
            pieces, blocks_w = [], []
            for b in range(3):
                for c in range(3):
                    at = (2 - a, 2 - b, 2 - c) if back else (a, b, c)
                    window = shifted[n, at[2], pl.ds(at[0], T), pl.ds(at[1], H)]
                    pieces.append(window.reshape(V, 2 * C))
                    w = w_split[filters, 9 * a + 3 * b + c]
                    if back:
                        high, low = w[:, :C], w[:, C:]
                        blocks_w.append(
                            jnp.concatenate(
                                [
                                    jnp.concatenate([high, high], axis=1),
                                    jnp.concatenate([low, low], axis=1),
                                ],
                                axis=0,
                            )
                        )
                    else:
                        blocks_w += [w, w]
            columns = jnp.concatenate(pieces, axis=1)
            if back:
                product = lax.dot_general(
                    columns, jnp.concatenate(blocks_w, axis=1), (((1,), (1,)), ((), ())),
                    preferred_element_type=f32,
                )
            else:
                product = jnp.dot(
                    columns, jnp.concatenate(blocks_w, axis=0), preferred_element_type=f32
                )
            if a == 0:
                acc[...] = product
            else:
                acc[...] += product
        return acc[:, :C] + acc[:, C:]

    def weight_grad(fixed, n, f):
        def taps(p, _):
            for m in range(9):
                q, c = m // 3, m % 3
                at = (p, q, c) if f else (2 - p, 2 - q, 2 - c)
                window = shifted[n, at[2], pl.ds(at[0], T), pl.ds(at[1], H)].reshape(V, 2 * C)
                o = jnp.dot(fixed[...], window, preferred_element_type=f32)
                o = (o[:C, :C] + o[C:, :C]) + (o[:C, C:] + o[C:, C:])
                raw[f, rows8((9 * p + m) * C, C)] = o.T if f else o
            return 0

        lax.fori_loop(0, 3, taps, 0)

    pieces = (
        (0, FIRST),
        (FIRST, SECOND),
        (FIRST + SECOND, SECOND),
        (FIRST + 2 * SECOND, THIRD),
        (FIRST + 2 * SECOND + THIRD, THIRD - 8),
    )

    def slots(kz, kx):
        return (
            (0, kz, kx * FIRST),
            (1, 2 * kx, kz * SECOND),
            (1, 2 * kx + 1, kz * SECOND),
            (2, 2 * kx, kz * THIRD),
            (2, 2 * kx + 1, kz * THIRD),
        )

    owners = [(kz, kx) for kz in range(4) for kx in range(2)]

    def core_swap(f):
        for kz, kx in owners:
            k = 4 * kz + 2 * kx + 1 - core
            for (start, size), (part, shard, to) in zip(pieces, slots(kz, kx)):
                pack[f, part, shard, to : to + size] = raw[f, rows8(OWN * k + start, size)]
            tail = (kz + 1) * THIRD - 8
            pack[f, 2, 2 * kx + 1, tail : tail + 8] = bias8[...] if f else jnp.zeros((8, C), f32)
        copy = remote(
            pack.at[f], summed.at[f], core_send.at[f], core_recv.at[f],
            (ta + 1 - 2 * core, ha, wa),
        )
        copy.start()
        return copy

    def core_add(f):
        for kz, kx in owners:
            k = 4 * kz + 2 * kx + core
            for (start, size), (part, shard, to) in zip(pieces, slots(kz, kx)):
                summed[f, part, shard, to : to + size] += raw[f, rows8(OWN * k + start, size)]
            if f:
                tail = (kz + 1) * THIRD - 8
                summed[f, 2, 2 * kx + 1, tail : tail + 8] += bias8[...]

    def line_start(f):
        for step in (2, 1, 3):
            for part, shard, device in (
                (0, zs[step], place(x, y, zs[step], core)),
                (1, ys[step], place(x, ys[step], z, core)),
                (2, xs[step], place(xs[step], y, z, core)),
            ):
                size = pl.ds(0, SHARD[part])
                remote(
                    summed.at[f, part, shard, size], line_recv.at[f, part, step - 1, size],
                    line_send.at[f, part], line_rcv.at[f, part], device,
                ).start()

    def line_take(f, sems):
        for part in range(3):
            take(line_recv.at[f, part, :, pl.ds(0, SHARD[part])], sems.at[f, part])

    def line_end(f):
        line_take(f, line_rcv)
        for part, own in ((0, z), (1, y), (2, x)):
            size = SHARD[part]
            line[f, part, :size] = (
                summed[f, part, own, :size] + line_recv[f, part, 0, :size]
            ) + (line_recv[f, part, 1, :size] + line_recv[f, part, 2, :size])

    def piece(part, one, two):
        if part == 0:
            return (two // 2) * FIRST + 16 * jnp.minimum(4 * lax.rem(two, 2) + one, 4)
        if part == 1:
            return two * SECOND + jnp.minimum(16 * one, SECOND - 16)
        return two * THIRD + jnp.minimum(16 * one, THIRD - 16)

    sides = ((xs, ys), (xs, zs), (ys, zs))

    def plane_start(f):
        copies = []
        for part in range(3):
            ones, twos = sides[part]
            mine = 4 * ones[0] + twos[0]
            for i, j in plane_xy:
                one, two = ones[i], twos[j]
                device = (
                    place(one, two, z, core),
                    place(one, y, two, core),
                    place(x, one, two, core),
                )[part]
                copy = remote(
                    line.at[f, part, rows8(piece(part, one, two), 16)],
                    plane_recv.at[f, part, mine],
                    plane_send.at[f, part], plane_rcv.at[f, part], device,
                )
                copies.append((-hops[i] - hops[j], len(copies), copy))
        for _, _, copy in sorted(copies, key=lambda entry: entry[:2]):
            copy.start()
        for part in range(3):
            ones, twos = sides[part]
            plane_recv[f, part, 4 * ones[0] + twos[0]] = line[
                f, part, rows8(piece(part, ones[0], twos[0]), 16)
            ]

    def plane_take(f, sems):
        for part in range(3):
            take(plane_recv.at[f, part, pl.ds(0, 15)], sems.at[f, part])

    def plane_end(f):
        plane_take(f, plane_rcv)
        for part in range(3):
            share[part, f] = jnp.sum(plane_recv[f, part], axis=0)

    halo_take(0, halo_recv)
    shift_columns(0)
    pre = conv(0, 0, False) + bias_v[...]
    pre_ref[...] = pre
    sig = 1.0 / (1.0 + jnp.exp(-pre))
    transposed(pre * sig, act_t)

    halo_take(1, halo_recv)
    shift_columns(1)
    weight_grad(act_t, 1, 0)
    swap0 = core_swap(0)

    grad_act = conv(1, 1, True)
    pre = pre_ref[...]
    sig = 1.0 / (1.0 + jnp.exp(-pre))
    grad_pre = grad_act * sig * (1.0 + pre * (1.0 - sig))
    bias8[...] = jnp.sum(grad_pre.reshape(V // 8, 8, C), axis=0)
    ext[2, pl.ds(0, T), pl.ds(1, H), pl.ds(LEFT, W)] = grad_pre.reshape(T, H, W, C)
    transposed(grad_pre, grad_t)

    swap0.wait_recv()
    core_add(0)
    line_start(0)

    def send_halo():
        plain.append(
            halo_plain(2, lambda t, h: ext.at[2, t, pl.ds(h.start + 1, h.size), pl.ds(LEFT, W)])
        )
        pack_columns(2)
        strips.append(halo_columns(2))
        for copy in strips[2] + plain[2]:
            copy.start()


    weight_grad(grad_t, 0, 1)
    swap1 = core_swap(1)
    swap1.wait_recv()
    core_add(1)
    line_start(1)

    send_halo()
    line_end(0)
    plane_start(0)

    def input_grad():
        gi_v[...] = conv(2, 0, True).reshape(T, H, W, C)
        gi_out.start()

    gi_out = pltpu.make_async_copy(gi_v, grad_input, local_sem.at[5])

    line_end(1)
    plane_start(1)

    for n in range(2):
        halo_take(n, halo_send)
    swap0.wait_send()
    swap1.wait_send()
    for f in range(2):
        line_take(f, line_send)
    plane_take(0, plane_send)
    plane_end(0)
    halo_take(2, halo_recv)
    shift_columns(2)
    plane_end(1)

    keeps = (
        (4 * lax.rem(y, 2) + x < 5,) * 2,
        (x < 2, x < 3),
        (y < 2, y + ha < 2),
    )
    squares = jnp.zeros((8, C), f32)
    for part in range(3):
        for half in range(2):
            mine = share[part, :, 8 * half : 8 * half + 8]
            squares += jnp.where(keeps[part][half], 1.0, 0.0) * jnp.sum(mine * mine, axis=0)
    note[0:1] = jnp.sum(squares, axis=0, keepdims=True)
    note[1:2] = jnp.sum(share[2, 1, 8:], axis=0, keepdims=True)
    here = 4 * x + y
    notes[here] = note[...]

    for i, j in plane_xy:
        remote(
            note, notes.at[here], n_send.at[0], n_recv.at[0], place(xs[i], ys[j], z, core)
        ).start()

    wide = y // 2
    half_slot = 4 * lax.rem(y, 2) + x

    def give(i, j):
        return remote(
            share.at[pl.ds(0, 2)], full.at[half_slot], ag_send.at[0], ag_recv.at[0],
            place(2 * wide + i, ys[j], z, core),
        )

    for j in (2, 1, 3, 0):
        for i in range(2):
            if j:
                give(i, j).start()
            else:

                @pl.when(2 * wide + i != x)
                def _(i=i):
                    give(i, 0).start()

    third_slot = 4 * ha + y
    for j in (2, 1, 3, 0):
        for row in (other, ha):
            if j or row is other:
                remote(
                    share.at[2], third.at[third_slot], ag_send.at[1], ag_recv.at[1],
                    (ta, row, ys[j]),
                ).start()
    third[third_slot] = share[2]

    @pl.when(wide == x_hi)
    def _():
        full[half_slot] = share[:2]

    input_grad()
    take(notes.at[pl.ds(0, 15)], n_recv.at[0])
    note2[0:1] = jnp.sum(notes[:, 0:1], axis=0)
    note2[1:2] = notes[5, 1:2]
    there = 2 * z + core
    notes2[there] = note2[...]
    for j, c in ((2, 1), (2, 0), (1, 1), (3, 1), (1, 0), (3, 0), (0, 1)):
        remote(
            note2, notes2.at[there], n_send.at[1], n_recv.at[1],
            place(x, y, zs[j], 1 - core if c else core),
        ).start()

    def shares_take(sems):
        sem = sems.at[0]
        take(third.at[pl.ds(0, 7)], sems.at[1])

        @pl.when(wide == x_hi)
        def _():
            take(full.at[pl.ds(0, 7)], sem)

        @pl.when(wide != x_hi)
        def _():
            take(full, sem)

    shares_take(ag_recv)
    shares_take(ag_send)
    plane_take(1, plane_send)
    take(notes.at[pl.ds(0, 15)], n_send.at[0])

    take(notes2.at[pl.ds(0, 7)], n_recv.at[1])
    everything = jnp.sum(notes2[:, 0:1], axis=0)
    raw_bias = notes2[0, 1:2]
    norm2 = jnp.sum(everything, axis=(0, 1), keepdims=True) + jnp.sum(
        raw_bias * raw_bias, axis=(0, 1), keepdims=True
    )
    factor = jnp.minimum(1.0, jnp.sqrt(jnp.full((1, 1), LIMIT, f32)) / jnp.sqrt(norm2))
    for f in range(2):
        out = g_v.at[f]
        for slot in range(8):
            half, at = slot // 4, 16 * (slot % 4)
            low = 16 * min(slot, 4)
            out[low : low + 16] = full[slot, 0, f] * factor
            low = FIRST + SECOND * half + min(at, SECOND - 16)
            out[low : low + 16] = full[slot, 1, f] * factor
            low = FIRST + 2 * SECOND + THIRD * half + min(at, THIRD - 16)
            size = min(16, OWN - low)
            out[low : low + size] = third[slot, f, :size] * factor
    gb_v[...] = raw_bias * factor
    lasts = [
        pltpu.make_async_copy(src, dst, local_sem.at[n])
        for n, (src, dst) in enumerate(
            ((g_v.at[1], grad_first), (g_v.at[0], grad_second), (gb_v, grad_bias))
        )
    ]
    for copy in lasts:
        copy.start()
    for copy in lasts + [gi_out]:
        copy.wait()

    take(notes2.at[pl.ds(0, 7)], n_send.at[1])
    halo_take(2, halo_send)


def hand_over(*refs):
    for source, out in zip(refs[:4], refs[4:]):
        out[...] = source[...]


def per_device(video_in, first_filter, first_bias, second_filter, grad_output):
    vmem = pltpu.VMEM
    dma = pltpu.SemaphoreType.DMA
    any_spec = pl.BlockSpec(memory_space=pl.ANY)
    vmem_spec = pl.BlockSpec(memory_space=pltpu.VMEM)
    shapes = (
        jax.ShapeDtypeStruct((T, H, W, C), f32),
        jax.ShapeDtypeStruct((OWN, C), f32),
        jax.ShapeDtypeStruct((OWN, C), f32),
        jax.ShapeDtypeStruct((1, C), f32),
    )
    outs = pl.pallas_call(
        kernel,
        out_shape=shapes,
        in_specs=[any_spec] * 5,
        out_specs=[any_spec] * 4,
        scratch_shapes=[
            vmem((2, 27, C, C), f32),
            vmem((2, 27, C, 2 * C), bf16),
            vmem((3, T + 2, H + 2, 32, C), f32),
            vmem((3, 2, T, H, 1, C), f32),
            vmem((3, 2, T + 2, H + 2, 1, C), f32),
            vmem((3, 3, T + 2, H + 2, W, 2 * C), bf16),
            vmem((V, 2 * C), f32),
            vmem((V, C), f32),
            vmem((2 * C, V), bf16),
            vmem((2 * C, V), bf16),
            vmem((2, ROWS, C), f32),
            vmem((8, C), f32),
            vmem((2, 3, 4, SHARD[0], C), f32),
            vmem((2, 3, 4, SHARD[0], C), f32),
            vmem((2, 3, 3, SHARD[0], C), f32),
            vmem((2, 3, SHARD[0], C), f32),
            vmem((2, 3, 16, 16, C), f32),
            vmem((3, 2, 16, C), f32),
            vmem((8, 2, 2, 16, C), f32),
            vmem((8, 2, 16, C), f32),
            vmem((2, C), f32),
            vmem((16, 2, C), f32),
            vmem((2, C), f32),
            vmem((8, 2, C), f32),
            vmem((1, C), f32),
            vmem((T, H, W, C), f32),
            vmem((2, OWN, C), f32),
            vmem((1, C), f32),
            dma((6,)),
            dma((3, 2)),
            dma((3, 2)),
            dma((2,)),
            dma((2,)),
            dma((2, 3)),
            dma((2, 3)),
            dma((2, 3)),
            dma((2, 3)),
            dma((2,)),
            dma((2,)),
            dma((2,)),
            dma((2,)),
        ],
        compiler_params=pltpu.CompilerParams(
            collective_id=0, has_side_effects=True, vmem_limit_bytes=56 * 1024 * 1024
        ),
        cost_estimate=pl.CostEstimate(
            flops=5 * 2 * V * ROWS * C, bytes_accessed=6 * 2**20, transcendentals=2 * V * C
        ),
    )(video_in, first_filter, first_bias.reshape(1, C), second_filter, grad_output)
    outs = pl.pallas_call(
        hand_over, out_shape=shapes, in_specs=[vmem_spec] * 4, out_specs=[vmem_spec] * 4
    )(*outs)
    grad_input, grad_first, grad_second, grad_bias = outs
    return grad_input, grad_first, grad_second, grad_bias.reshape(C)


def solution(mesh):
    placed = (P("ta", "ha", "wa", None), P(), P(), P(), P("ta", "ha", "wa", None))
    return jax.shard_map(
        per_device,
        mesh=mesh,
        in_specs=placed,
        out_specs=(P("ta", "ha", "wa", None), P("ta", None), P("ta", None), P()),
        check_vma=False,
    )
```
